256 devices in a mesh: dp: 32 (over y, x, z_lo), tensor: 8 (over z_hi, core).
Axes of the slice: x: 4, y: 4, z: 8 (z_hi: 4, z_lo: 2; z = z_hi * 2 + z_lo), core: 2. Of those that a mesh axis runs over, the one named last changes fastest.
Arguments:
- queries: bfloat16 [22528, 4096], P('dp', 'tensor'), may hold values from -6 to 6
- nb_states: bfloat16 [512, 128, 768], P('dp', 'tensor'), may hold values from -400 to 400
- nb_owner: int32 [352, 2], P('dp'), may hold values from 0 to 31, all different within a row; in each aligned block of 11 rows (0 to 10, 11 to 21, ...) at most 2 rows name the same one
- nb_row: int32 [352, 2], P('dp'), may hold values from 0 to 15
- enc_gain: float32 [768], replicated, may hold values from 0.1 to 1.9
- key_weight: bfloat16 [768, 4096], P(None, 'tensor'), may hold values from -0.21875 to 0.21875
- value_weight: bfloat16 [768, 4096], P(None, 'tensor'), may hold values from -0.21875 to 0.21875
- grad_attn: bfloat16 [22528, 4096], P('dp', 'tensor'), may hold values from -3 to 3
Outputs:
- attn_out: bfloat16 [22528, 4096], P('dp', 'tensor')
- grad_queries: bfloat16 [22528, 4096], P('dp', 'tensor')
- grad_states: bfloat16 [512, 128, 768], P('dp', 'tensor')
- grad_key_weight: float32 [768, 4096], P(None, 'tensor')
- grad_value_weight: float32 [768, 4096], P(None, 'tensor')
The draws below stay inside these ranges and needn't reach their ends.
Inputs may be any that keep to these rules, and one draw needn't show every extreme that they name: `nb_owner`: the 2 neighbours of a span have different owners; among the 11 spans of one dp index no owner is named more than 2 times, a bound that some block reaches.
All inputs are finite; a program needn't handle non-finite values.
Results may differ from the reference program's by a relative error of at most 0.03.
Values may be sent and summed in bfloat16 or wider, within the bound.
A program may use at most 128 MiB of HBM per device.

```python
import math
import jax
import jax.numpy as jnp
import numpy as np
from jax import lax

ENC_D = 768
HEADS = 32
HEAD_DIM = 128
SPAN = 64
NB_LEN = 128
NBR = 2
CH_DEV = 11
SLOT_CAP = 2
NB_DEV = 16
ATT = 4096
SPANS = 352
TOKENS = 22528
NB_ALL = 512
N_DP = 32
N_TENSOR = 8


def draw_nb_states(key, part):
    base_key, row_key, col_key = jax.random.split(key, 3)
    full_shape = (NB_ALL, NB_LEN, ENC_D)
    row_scale = jnp.exp(jax.random.uniform(row_key, (NB_ALL, NB_LEN, 1), jnp.float32, 0.0, math.log(10.0)))
    col_scale = jnp.exp(jax.random.uniform(col_key, (1, 1, ENC_D), jnp.float32, 0.0, math.log(10.0)))
    base_values = jnp.clip(jax.random.normal(base_key, full_shape, jnp.float32), -4.0, 4.0)
    return (base_values * row_scale * col_scale).astype(jnp.bfloat16)


def plant(array, key, smallest, largest):
    extent = array.shape
    place = [jax.random.randint(jax.random.fold_in(key, axis), (), 0, extent[axis]) for axis in range(len(extent))]
    array = array.at[tuple(place)].set(smallest)
    longest = extent.index(max(extent))
    place[longest] = (place[longest] + 1) % extent[longest]
    return array.at[tuple(place)].set(largest)


def shard_levels(own_key, extent, cuts, smallest, top_value):
    def one(dim, blocks):
        heights = jax.random.uniform(jax.random.fold_in(jax.random.fold_in(own_key, 6), dim), (blocks,), jnp.float32, smallest / len(cuts), top_value / len(cuts))
        return jnp.repeat(jnp.exp(heights), extent[dim] // blocks).reshape((-1,) + (1,) * (len(extent) - dim - 1))

    gain = one(*cuts[0])
    for cut in cuts[1:]:
        gain = gain * one(*cut)
    return gain


def routed_block(key, own, number, rows, count, top, bound, skew):
    order = jax.random.permutation(key, count)
    packed, usual = load_shares(count, rows * top, bound, skew, True), load_shares(count, rows * top, bound, skew, False)
    places = jnp.arange(count)

    def named(sizes, rotation):
        used = int((sizes > 0).sum())
        fixed = max(1, used // 4)
        moved = fixed + (places - fixed + rotation * (used - fixed)) % max(1, count - fixed)
        return jnp.zeros((count,), jnp.int32).at[order[jnp.where(places < fixed, places, moved)]].set(jnp.asarray(sizes, jnp.int32))

    sizes = jnp.where(number % 4 == 0, named(packed, number // 4), named(usual, number - number // 4 - 1))
    mixed = jax.random.permutation(jax.random.fold_in(own, 3), count)
    source_of, receiver = mixed[0:count // 2 * 2:2], mixed[1:count // 2 * 2:2]
    margin = jnp.minimum(sizes[source_of] - 1, bound - sizes[receiver]) // 2
    margin = jnp.where((source_of == order[0]) | (receiver == order[0]) | (sizes[receiver] == 0), 0, jnp.maximum(margin, 0))
    moved = jax.random.randint(jax.random.fold_in(own, 4), (count // 2,), 0, 1 << 20) % (margin + 1)
    sizes = sizes.at[source_of].add(-moved).at[receiver].add(moved)
    labels = jnp.searchsorted(jnp.cumsum(sizes), jnp.arange(rows * top), side="right").astype(jnp.int32)
    table = labels.reshape(top, rows).T
    table = table[jax.random.permutation(jax.random.fold_in(own, 1), rows)]
    rotation = jax.random.randint(jax.random.fold_in(own, 2), (rows, 1), 0, top)
    return jnp.take_along_axis(table, (jnp.arange(top)[None, :] + rotation) % top, axis=1)


def load_shares(number_of, total, limit, slope, full):
    weights = [(1 << 20) // math.isqrt(grade ** slope) + 1 for grade in range(1, number_of + 1)]
    largest = limit if full else min(limit, max(-(-total // number_of), total * weights[0] // sum(weights)))
    least = 1 if total - largest >= number_of - 1 else 0
    holding, surplus = [largest] + [least] * (number_of - 1), total - largest - least * (number_of - 1)
    while surplus > 0:
        candidates = [i for i in range(1, number_of) if holding[i] < largest] or [i for i in range(1, number_of) if holding[i] < limit]
        pool, budget = sum([weights[i] for i in candidates]), surplus
        for i in candidates:
            more = min(limit - holding[i], max(1, budget * weights[i] // pool), surplus)
            holding[i] = holding[i] + more
            surplus = surplus - more
    return np.array(holding)


def centred(stream_key, shape, width, reach, shards=(), dtype=jnp.bfloat16):
    values = width * jax.random.normal(stream_key, shape, jnp.float32)
    if shards:
        values = values * shard_levels(stream_key, shape, shards, -0.22, 0.18)
    return jnp.clip(values, -reach, reach).astype(dtype)


def setup_inputs(seed: int = 0) -> dict:
    key_list = jax.random.split(jax.random.key(seed), 9)
    queries = centred(key_list[0], (TOKENS, ATT), 1.0, 6.0, ((0, 32), (1, 8)))
    nb_states = draw_nb_states(jax.random.fold_in(key_list[8], 71), 0)
    nb_owner_keys = jax.random.split(jax.random.fold_in(key_list[2], 1), SPANS // CH_DEV)
    nb_owner_turns = jax.random.permutation(jax.random.fold_in(key_list[2], 3), SPANS // CH_DEV)
    nb_owner = jax.vmap(lambda own, number: routed_block(jax.random.fold_in(key_list[2], 2), own, number, CH_DEV, N_DP, NBR, SLOT_CAP, 2))(nb_owner_keys, nb_owner_turns).reshape((SPANS, NBR))
    nb_row = plant(jax.random.randint(key_list[3], (SPANS, NBR), 0, NB_DEV), jax.random.fold_in(key_list[3], 1), 0, NB_DEV - 1).astype(jnp.int32)
    enc_gain = jnp.clip(1.0 + 0.18 * jax.random.normal(key_list[4], (ENC_D,), jnp.float32), 0.1, 1.9)
    key_weight = centred(key_list[5], (ENC_D, ATT), ENC_D ** -0.5, 0.21875, ((1, 8),))
    value_weight = centred(key_list[6], (ENC_D, ATT), ENC_D ** -0.5, 0.21875, ((1, 8),))
    grad_attn = centred(key_list[7], (TOKENS, ATT), 0.5, 3.0, ((0, 32), (1, 8)))
    return {"queries": queries, "nb_states": nb_states, "nb_owner": nb_owner, "nb_row": nb_row, "enc_gain": enc_gain, "key_weight": key_weight, "value_weight": value_weight, "grad_attn": grad_attn}


epsilon = 1e-06

def normalize(values):
    widened = values.astype(jnp.float32)
    inverse = lax.rsqrt(lax.optimization_barrier(jnp.mean(widened * widened, axis=-1, keepdims=True)) + epsilon)
    return (widened * inverse, inverse)

def reference(queries, nb_states, nb_owner, nb_row, enc_gain, key_weight, value_weight, grad_attn):
    flat_index = (nb_owner * NB_DEV + nb_row).astype(jnp.int32).reshape(N_DP, CH_DEV * NBR)
    query_groups = queries.reshape(N_DP, CH_DEV, SPAN, HEADS, HEAD_DIM)
    grad_groups = grad_attn.reshape(N_DP, CH_DEV, SPAN, HEADS, HEAD_DIM)
    gain_wide = enc_gain.astype(jnp.float32)
    score_scale = HEAD_DIM ** (-0.5)
    group_cols = ATT // N_TENSOR

    def one_group(totals, group_item):
        index_row, query_blocks, grad_blocks = group_item
        raw_states = nb_states[index_row]
        unit_states, inverse = normalize(raw_states)
        encoded = (unit_states * gain_wide).astype(jnp.bfloat16)
        flat_encoded = encoded.reshape(CH_DEV * NBR * NB_LEN, ENC_D)
        key_all = jnp.dot(flat_encoded, key_weight, preferred_element_type=jnp.float32).astype(jnp.bfloat16)
        value_all = jnp.dot(flat_encoded, value_weight, preferred_element_type=jnp.float32).astype(jnp.bfloat16)
        key_blocks = key_all.reshape(CH_DEV, NBR * NB_LEN, HEADS, HEAD_DIM).astype(jnp.float32)
        value_blocks = value_all.reshape(CH_DEV, NBR * NB_LEN, HEADS, HEAD_DIM).astype(jnp.float32)
        query_wide = query_blocks.astype(jnp.float32)
        grad_wide = grad_blocks.astype(jnp.float32)
        scores = jnp.einsum('cqhd,ckhd->chqk', query_wide, key_blocks) * score_scale
        exponent = jnp.exp(scores)
        probabilities = exponent / lax.optimization_barrier(jnp.sum(exponent, axis=-1, keepdims=True))
        weights = probabilities.astype(jnp.bfloat16)
        weights_wide = weights.astype(jnp.float32)
        attention = jnp.einsum('chqk,ckhd->cqhd', weights_wide, value_blocks).astype(jnp.bfloat16)
        grad_weights = jnp.einsum('cqhd,ckhd->chqk', grad_wide, value_blocks)
        grad_scores = (probabilities * (grad_weights - lax.optimization_barrier(jnp.sum(probabilities * grad_weights, axis=-1, keepdims=True))) * score_scale).astype(jnp.bfloat16)
        grad_scores_wide = grad_scores.astype(jnp.float32)
        grad_query = jnp.einsum('chqk,ckhd->cqhd', grad_scores_wide, key_blocks).astype(jnp.bfloat16)
        grad_keys = jnp.einsum('chqk,cqhd->ckhd', grad_scores_wide, query_wide).astype(jnp.bfloat16).reshape(-1, ATT)
        grad_values = jnp.einsum('chqk,cqhd->ckhd', weights_wide, grad_wide).astype(jnp.bfloat16).reshape(-1, ATT)
        totals_next = (totals[0] + jnp.dot(flat_encoded.T, grad_keys, preferred_element_type=jnp.float32), totals[1] + jnp.dot(flat_encoded.T, grad_values, preferred_element_type=jnp.float32))
        enc_total = jnp.zeros((CH_DEV * NBR * NB_LEN, ENC_D), jnp.float32)
        for share_index in range(N_TENSOR):
            column_range = slice(share_index * group_cols, (share_index + 1) * group_cols)
            partial_term = jnp.dot(grad_keys[:, column_range], key_weight[:, column_range].T, preferred_element_type=jnp.float32)
            partial_term = partial_term + jnp.dot(grad_values[:, column_range], value_weight[:, column_range].T, preferred_element_type=jnp.float32)
            rounded = lax.optimization_barrier(partial_term.astype(jnp.bfloat16))
            enc_total = enc_total + rounded.astype(jnp.float32)
        scaled = enc_total.reshape(CH_DEV * NBR, NB_LEN, ENC_D) * gain_wide
        grad_raw = (inverse * (scaled - unit_states * lax.optimization_barrier(jnp.mean(scaled * unit_states, axis=-1, keepdims=True)))).astype(jnp.bfloat16)
        return (totals_next, (attention, grad_query, grad_raw))
    start_totals = (jnp.zeros((ENC_D, ATT), jnp.float32), jnp.zeros((ENC_D, ATT), jnp.float32))
    totals_end, stacked = lax.scan(one_group, start_totals, (flat_index, query_groups, grad_groups))
    attn_out = stacked[0].reshape(TOKENS, ATT)
    grad_queries = stacked[1].reshape(TOKENS, ATT)
    grad_raw_all = stacked[2].reshape(SPANS * NBR, NB_LEN, ENC_D).astype(jnp.float32)
    grad_states = jnp.zeros((NB_ALL, NB_LEN, ENC_D), jnp.float32).at[flat_index.reshape(-1)].add(grad_raw_all)
    return (attn_out, grad_queries, grad_states.astype(jnp.bfloat16), totals_end[0], totals_end[1])
```

```python
import jax
import jax.numpy as jnp
from jax import lax
from jax.sharding import PartitionSpec as P

HEAD_DIM = 128


epsilon = 1e-06


def normalize(values):
    widened = values.astype(jnp.float32)
    inverse = lax.rsqrt(jnp.mean(widened * widened, axis=-1, keepdims=True) + epsilon)
    return (widened * inverse, inverse)


def body(queries, nb_states, nb_owner, nb_row, enc_gain, key_weight, value_weight, grad_attn):
    groups = lax.axis_size("dp")
    owner_list = nb_owner.reshape(-1)
    row_list = nb_row.reshape(-1)
    asked_count = owner_list.shape[0]
    capacity = max(2, (2 * asked_count + groups - 1) // groups)
    positions = jnp.arange(asked_count, dtype=jnp.int32)
    same_owner = owner_list[:, None] == owner_list[None, :]
    before_me = positions[None, :] < positions[:, None]
    slot_rank = jnp.sum(jnp.where(same_owner & before_me, 1, 0), axis=1).astype(jnp.int32)
    slot_index = owner_list * capacity + slot_rank
    slot_count = groups * capacity
    selector = slot_index[:, None] == jnp.arange(slot_count, dtype=jnp.int32)[None, :]
    request = jnp.sum(jnp.where(selector, row_list[:, None], 0), axis=0).reshape(groups, capacity)
    asked_rows = lax.all_to_all(request, "dp", split_axis=0, concat_axis=0, tiled=True)
    asked_flat = asked_rows.reshape(-1)
    local_len = nb_states.shape[1]
    enc_width = nb_states.shape[2]
    outgoing = nb_states[asked_flat].reshape(groups, capacity, local_len, enc_width)
    fetched = lax.all_to_all(outgoing, "dp", split_axis=0, concat_axis=0, tiled=True)
    select_half = selector.astype(jnp.bfloat16)
    mine_states = jnp.dot(
        select_half,
        fetched.reshape(slot_count, local_len * enc_width),
        preferred_element_type=jnp.float32,
    )
    mine_states = mine_states.astype(jnp.bfloat16).reshape(asked_count, local_len, enc_width)
    unit_slice, inverse_slice = normalize(mine_states)
    gathered = lax.all_gather(mine_states, "tensor", axis=1, tiled=True)
    unit_all, inverse_all = normalize(gathered)
    encoded = (unit_all * enc_gain).astype(jnp.bfloat16)
    full_len = encoded.shape[1]
    flat_encoded = encoded.reshape(asked_count * full_len, enc_width)
    key_all = jnp.dot(flat_encoded, key_weight, preferred_element_type=jnp.float32).astype(
        jnp.bfloat16
    )
    value_all = jnp.dot(flat_encoded, value_weight, preferred_element_type=jnp.float32).astype(
        jnp.bfloat16
    )
    span_count = nb_owner.shape[0]
    per_span = nb_owner.shape[1]
    heads_here = key_weight.shape[1] // HEAD_DIM
    span_len = queries.shape[0] // span_count
    key_blocks = key_all.reshape(span_count, per_span * full_len, heads_here, HEAD_DIM)
    value_blocks = value_all.reshape(span_count, per_span * full_len, heads_here, HEAD_DIM)
    query_blocks = queries.reshape(span_count, span_len, heads_here, HEAD_DIM)
    grad_blocks = grad_attn.reshape(span_count, span_len, heads_here, HEAD_DIM)
    score_scale = HEAD_DIM ** (-0.5)
    scores = (
        jnp.einsum("cqhd,ckhd->chqk", query_blocks, key_blocks, preferred_element_type=jnp.float32)
        * score_scale
    )
    exponent = jnp.exp(scores)
    probabilities = exponent / jnp.sum(exponent, axis=-1, keepdims=True)
    weights = probabilities.astype(jnp.bfloat16)
    attn_out = jnp.einsum(
        "chqk,ckhd->cqhd", weights, value_blocks, preferred_element_type=jnp.float32
    )
    attn_out = attn_out.astype(jnp.bfloat16).reshape(queries.shape)
    grad_weights = jnp.einsum(
        "cqhd,ckhd->chqk", grad_blocks, value_blocks, preferred_element_type=jnp.float32
    )
    grad_scores = (
        probabilities
        * (grad_weights - jnp.sum(probabilities * grad_weights, axis=-1, keepdims=True))
        * score_scale
    ).astype(jnp.bfloat16)
    grad_queries = jnp.einsum(
        "chqk,ckhd->cqhd", grad_scores, key_blocks, preferred_element_type=jnp.float32
    )
    grad_queries = grad_queries.astype(jnp.bfloat16).reshape(queries.shape)
    grad_keys = jnp.einsum(
        "chqk,cqhd->ckhd", grad_scores, query_blocks, preferred_element_type=jnp.float32
    )
    grad_keys = grad_keys.astype(jnp.bfloat16).reshape(-1, key_weight.shape[1])
    grad_values = jnp.einsum(
        "chqk,cqhd->ckhd", weights, grad_blocks, preferred_element_type=jnp.float32
    )
    grad_values = grad_values.astype(jnp.bfloat16).reshape(-1, value_weight.shape[1])
    key_term = jnp.dot(flat_encoded.T, grad_keys, preferred_element_type=jnp.float32)
    value_term = jnp.dot(flat_encoded.T, grad_values, preferred_element_type=jnp.float32)
    terms = jnp.concatenate([key_term, value_term], axis=0).astype(jnp.bfloat16)
    piece_rows = terms.shape[0] // groups
    terms = terms.reshape(groups, piece_rows, key_weight.shape[1])
    pieces = lax.all_to_all(terms, "dp", split_axis=0, concat_axis=0, tiled=True)
    piece = jnp.sum(pieces.astype(jnp.float32), axis=0, keepdims=True).astype(jnp.bfloat16)
    whole = lax.all_to_all(
        jnp.broadcast_to(piece, terms.shape), "dp", split_axis=0, concat_axis=0, tiled=True
    )
    whole = whole.reshape(2, enc_width, key_weight.shape[1]).astype(jnp.float32)
    grad_key_weight, grad_value_weight = whole[0], whole[1]
    enc_term = jnp.dot(grad_keys, key_weight.T, preferred_element_type=jnp.float32)
    enc_term = enc_term + jnp.dot(grad_values, value_weight.T, preferred_element_type=jnp.float32)
    tensor_count = lax.axis_size("tensor")
    enc_term = enc_term.astype(jnp.bfloat16).reshape(asked_count, tensor_count, local_len, enc_width)
    enc_parts = lax.all_to_all(
        enc_term.transpose(1, 0, 2, 3), "tensor", split_axis=0, concat_axis=0, tiled=True
    )
    own_grad = jnp.sum(enc_parts.astype(jnp.float32), axis=0)
    scaled = own_grad * enc_gain
    grad_raw = (
        inverse_slice
        * (scaled - unit_slice * jnp.mean(scaled * unit_slice, axis=-1, keepdims=True))
    ).astype(jnp.bfloat16)
    outgoing_grad = jnp.dot(
        select_half.T,
        grad_raw.reshape(asked_count, local_len * enc_width),
        preferred_element_type=jnp.float32,
    )
    outgoing_grad = outgoing_grad.astype(jnp.bfloat16).reshape(
        groups, capacity, local_len, enc_width
    )
    returned = lax.all_to_all(outgoing_grad, "dp", split_axis=0, concat_axis=0, tiled=True)
    owned_count = nb_states.shape[0]
    owner_rows = (asked_flat[None, :] == jnp.arange(owned_count, dtype=jnp.int32)[:, None]).astype(
        jnp.bfloat16
    )
    grad_states = jnp.dot(
        owner_rows,
        returned.reshape(slot_count, local_len * enc_width),
        preferred_element_type=jnp.float32,
    )
    grad_states = grad_states.astype(jnp.bfloat16).reshape(nb_states.shape)
    return (attn_out, grad_queries, grad_states, grad_key_weight, grad_value_weight)


def solution(mesh):
    return jax.shard_map(
        body,
        mesh=mesh,
        in_specs=(
            P("dp", "tensor"),
            P("dp", "tensor", None),
            P("dp", None),
            P("dp", None),
            P(),
            P(None, "tensor"),
            P(None, "tensor"),
            P("dp", "tensor"),
        ),
        out_specs=(
            P("dp", "tensor"),
            P("dp", "tensor"),
            P("dp", "tensor", None),
            P(None, "tensor"),
            P(None, "tensor"),
        ),
        check_vma=False,
    )
```

```python
import jax
import jax.numpy as jnp
from jax import lax
from jax.experimental import pallas as pl
from jax.experimental.pallas import tpu as pltpu
from jax.sharding import PartitionSpec as P

HEAD_DIM = 128
MESH = pl.DeviceIdType.MESH
SCALE = HEAD_DIM ** (-0.5)
RINGS = 4
F32 = jnp.float32
BF16 = jnp.bfloat16

epsilon = 1e-06


def normalize(values):
    widened = values.astype(F32)
    inverse = lax.rsqrt(jnp.mean(widened * widened, axis=-1, keepdims=True) + epsilon)
    return (widened * inverse, inverse)


def dot(a, b, ca, cb):
    return lax.dot_general(a, b, (((ca,), (cb,)), ((), ())), preferred_element_type=F32)


def drain(ref, sem):
    pltpu.make_async_copy(ref, ref, sem).wait()


def send(src, dst, send_sem, recv_sem, device):
    pltpu.make_async_remote_copy(
        src_ref=src,
        dst_ref=dst,
        send_sem=send_sem,
        recv_sem=recv_sem,
        device_id=device,
        device_id_type=MESH,
    ).start()


def layer_kernel(
    spans,
    per,
    places,
    mine,
    queries,
    grads,
    gain,
    key_w,
    value_w,
    attn_out,
    grad_q,
    grad_raw,
    grad_w,
    full,
    enc_t,
    grad_kv,
    term,
    from_core,
    sums,
    near_a,
    near_b,
    far_a,
    far_b,
    w_terms,
    w_slots,
    w_half,
    w_other,
    w_mine,
    w_back,
    left_sem,
    right_sem,
    half_sem,
    core_sem,
    swap_sem,
    first_sem,
    second_sem,
    w_sem,
    out_sem,
):
    me_dp = lax.axis_index("dp")
    me_t = lax.axis_index("tensor")
    ring, core = me_t // 2, lax.rem(me_t, 2)
    place, low = me_dp // 2, lax.rem(me_dp, 2)
    r_ring, l_ring, o_ring = (lax.rem(ring + d, RINGS) for d in (1, 3, 2))
    right = {"tensor": r_ring * 2 + core}
    left = {"tensor": l_ring * 2 + core}
    twin = {"tensor": ring * 2 + 1 - core}
    mate = {"dp": place * 2 + 1 - low}

    def place_at(k):
        return lax.rem(place + k, places)

    barrier = pltpu.get_barrier_semaphore()
    for device in (right, left, twin, mate):
        pl.semaphore_signal(barrier, inc=1, device_id=device, device_id_type=MESH)

    def greet(k, carry):
        device = {"dp": place_at(k) * 2 + low}
        pl.semaphore_signal(barrier, inc=1, device_id=device, device_id_type=MESH)
        return carry

    lax.fori_loop(1, places, greet, 0)
    pl.semaphore_wait(barrier, 4 + places - 1)

    gain_row = gain[...]
    span_len = queries.shape[0] // spans
    local_len, width = mine.shape[1], mine.shape[2]
    tokens = per * 2 * RINGS * local_len
    cols = queries.shape[1]

    def rows_of(c):
        return pl.ds(c * per, per)

    def gather_step(i, carry):
        @pl.when(i < spans)
        def _():
            at = rows_of(i)
            here = full.at[at, ring, core]
            block = mine.at[at]
            send(block, here, out_sem.at[0], left_sem.at[i], right)
            send(block, here, out_sem.at[1], right_sem.at[i], left)
            send(block, here, out_sem.at[2], core_sem.at[i], twin)
            full[at, ring, core] = mine[at]

        j = i - 2

        @pl.when((j >= 0) & (j < spans))
        def _():
            at = rows_of(j)
            from_left = full.at[at, l_ring, core]
            from_right = full.at[at, r_ring, core]
            drain(from_left, left_sem.at[j])
            one = full.at[j * per, l_ring, core]
            send(one, one, out_sem.at[3], half_sem.at[j], right)
            send(from_left, from_left, out_sem.at[5], core_sem.at[j], twin)
            drain(from_right, right_sem.at[j])
            two = full.at[j * per + 1, r_ring, core]
            send(two, two, out_sem.at[4], half_sem.at[j], left)
            send(from_right, from_right, out_sem.at[6], core_sem.at[j], twin)

        k = i - 4

        @pl.when((k >= 0) & (k < spans))
        def _():
            across = full.at[rows_of(k), o_ring, core]
            drain(across, half_sem.at[k])
            send(across, across, out_sem.at[7], core_sem.at[k], twin)

        c = i - 5

        @pl.when(c >= 0)
        def _():
            at = rows_of(c)
            drain(full.at[at, :, 1 - core], core_sem.at[c])
            unit, _ = normalize(full[at].reshape(tokens, width))
            encoded = (unit * gain_row).astype(BF16)
            enc_t[:, pl.ds(pl.multiple_of(c * tokens, tokens), tokens)] = encoded.T
            keys = dot(encoded, key_w[...], 1, 0).astype(BF16)
            values = dot(encoded, value_w[...], 1, 0).astype(BF16)
            q_rows = pl.ds(pl.multiple_of(c * span_len, span_len), span_len)
            t_rows = pl.ds(pl.multiple_of(c * tokens, tokens), tokens)
            for h in range(cols // HEAD_DIM):
                lanes = slice(h * HEAD_DIM, (h + 1) * HEAD_DIM)
                q, g = queries[q_rows, lanes], grads[q_rows, lanes]
                kh, vh = keys[:, lanes], values[:, lanes]
                exponent = jnp.exp(dot(q, kh, 1, 1) * SCALE)
                p = exponent / jnp.sum(exponent, axis=-1, keepdims=True)
                w = p.astype(BF16)
                attn_out[q_rows, lanes] = dot(w, vh, 1, 0).astype(BF16)
                gw = dot(g, vh, 1, 1)
                gs = (p * (gw - jnp.sum(p * gw, axis=-1, keepdims=True)) * SCALE).astype(BF16)
                grad_q[q_rows, lanes] = dot(gs, kh, 1, 0).astype(BF16)
                grad_kv[t_rows, lanes] = dot(gs, q, 0, 0).astype(BF16)
                v_lanes = slice(cols + h * HEAD_DIM, cols + (h + 1) * HEAD_DIM)
                grad_kv[t_rows, v_lanes] = dot(w, g, 0, 0).astype(BF16)

        return carry

    lax.fori_loop(0, spans + 5, gather_step, 0)

    tile = 256
    tiles = width // tile
    for part in range(2):

        def weight_step(r, carry, part=part):
            left_side = enc_t[pl.ds(pl.multiple_of(r * tile, tile), tile), :]
            product = dot(left_side, grad_kv[:, part * cols : (part + 1) * cols], 1, 0)
            row = pl.multiple_of(part * width + r * tile, tile)
            w_terms[pl.ds(row, tile), :] = product.astype(BF16)
            return carry

        lax.fori_loop(0, tiles, weight_step, 0)

    piece = w_slots.shape[1]
    half = piece // 2

    def piece_rows(p):
        return pl.ds(pl.multiple_of(p * piece, piece), piece)

    def scatter(k, carry):
        p = place_at(k)
        send(
            w_terms.at[piece_rows(p)],
            w_slots.at[k - 1],
            out_sem.at[8],
            w_sem.at[0],
            {"dp": p * 2 + low},
        )
        return carry

    lax.fori_loop(1, places, scatter, 0)

    def reduce_step(i, carry):
        @pl.when(i < spans)
        def _():
            t_rows = pl.ds(pl.multiple_of(i * tokens, tokens), tokens)
            product = dot(grad_kv[t_rows, :cols], key_w[...], 1, 1)
            product = product + dot(grad_kv[t_rows, cols:], value_w[...], 1, 1)
            at = rows_of(i)
            term[at] = product.astype(BF16).reshape(per, RINGS, 2, local_len, width)
            send(
                term.at[at, :, 1 - core],
                from_core.at[at],
                out_sem.at[9],
                swap_sem.at[i],
                twin,
            )

        j = i - 1

        @pl.when((j >= 0) & (j < spans))
        def _():
            at = rows_of(j)
            drain(from_core.at[at], swap_sem.at[j])
            total = term[at, :, core].astype(F32) + from_core[at].astype(F32)
            sums[at] = total.astype(BF16)
            send(sums.at[j * per, o_ring], near_a.at[j], out_sem.at[10], first_sem.at[0, j], right)
            send(
                sums.at[j * per + 1, o_ring], near_b.at[j], out_sem.at[11], first_sem.at[1, j], left
            )

        k = i - 3

        @pl.when((k >= 0) & (k < spans))
        def _():
            at = rows_of(k)
            drain(near_a.at[k], first_sem.at[0, k])
            total = sums[k * per, r_ring].astype(F32) + near_a[k].astype(F32)
            sums[k * per, r_ring] = total.astype(BF16)
            send(sums.at[at, r_ring], far_a.at[at], out_sem.at[12], second_sem.at[0, k], right)
            drain(near_b.at[k], first_sem.at[1, k])
            total = sums[k * per + 1, l_ring].astype(F32) + near_b[k].astype(F32)
            sums[k * per + 1, l_ring] = total.astype(BF16)
            send(sums.at[at, l_ring], far_b.at[at], out_sem.at[13], second_sem.at[1, k], left)

        @pl.when(i == 7)
        def _():
            drain(w_slots, w_sem.at[0])
            total = w_terms[piece_rows(place), :].astype(F32)
            for s in range(places - 1):
                total = total + w_slots[s].astype(F32)
            w_half[...] = total.astype(BF16).reshape(2, half, cols)
            send(w_half.at[1 - low], w_other, out_sem.at[14], w_sem.at[1], mate)

        @pl.when(i == 8)
        def _():
            drain(w_other, w_sem.at[1])
            total = w_half[low].astype(F32) + w_other[...].astype(F32)
            w_mine[low] = total.astype(BF16)
            send(w_mine.at[low], w_mine.at[low], out_sem.at[15], w_sem.at[2], mate)

        @pl.when(i == 9)
        def _():
            drain(w_mine.at[1 - low], w_sem.at[2])

            def spread(k, carry):
                device = {"dp": place_at(k) * 2 + low}
                send(w_mine, w_back.at[k - 1], out_sem.at[16], w_sem.at[3], device)
                return carry

            lax.fori_loop(1, places, spread, 0)

        c = i - 5

        @pl.when(c >= 0)
        def _():
            at = rows_of(c)
            drain(far_a.at[at], second_sem.at[0, c])
            drain(far_b.at[at], second_sem.at[1, c])
            own = sums[at, ring].astype(F32) + far_a[at].astype(F32) + far_b[at].astype(F32)
            own = own.reshape(per * local_len, width)
            unit, inverse = normalize(mine[at].reshape(per * local_len, width))
            scaled = own * gain_row
            raw = inverse * (scaled - unit * jnp.mean(scaled * unit, axis=-1, keepdims=True))
            grad_raw[at] = raw.astype(BF16).reshape(per, local_len, width)

        return carry

    lax.fori_loop(0, spans + 5, reduce_step, 0)

    drain(w_back, w_sem.at[3])
    grad_w[place] = w_mine[...].reshape(piece, cols).astype(F32)

    def widen(k, carry):
        source = lax.rem(place + places - k, places)
        grad_w[source] = w_back[k - 1].reshape(piece, cols).astype(F32)
        return carry

    lax.fori_loop(1, places, widen, 0)

    for n in (0, 1, 2, 5, 6, 7):
        drain(mine, out_sem.at[n])
    drain(near_a, out_sem.at[3])
    drain(near_a, out_sem.at[4])
    drain(w_slots, out_sem.at[8])
    drain(from_core, out_sem.at[9])
    drain(near_a, out_sem.at[10])
    drain(near_b, out_sem.at[11])
    drain(far_a, out_sem.at[12])
    drain(far_b, out_sem.at[13])
    drain(w_other, out_sem.at[14])
    drain(w_other, out_sem.at[15])
    drain(w_back, out_sem.at[16])


def layer(mine_states, queries, grad_attn, enc_gain, key_weight, value_weight, spans, groups):
    asked, local_len, width = mine_states.shape
    per = asked // spans
    rows, cols = queries.shape
    places = groups // 2
    tokens = asked * local_len * RINGS * 2
    piece = 2 * width // places

    def kernel(*refs):
        layer_kernel(spans, per, places, *refs)

    vmem = pl.BlockSpec(memory_space=pltpu.VMEM)
    dma = pltpu.SemaphoreType.DMA
    return pl.pallas_call(
        kernel,
        out_shape=(
            jax.ShapeDtypeStruct((rows, cols), BF16),
            jax.ShapeDtypeStruct((rows, cols), BF16),
            jax.ShapeDtypeStruct((asked, local_len, width), BF16),
            jax.ShapeDtypeStruct((places, piece, cols), F32),
        ),
        in_specs=[vmem] * 6,
        out_specs=(vmem,) * 4,
        scratch_shapes=[
            pltpu.VMEM((asked, RINGS, 2, local_len, width), BF16),
            pltpu.VMEM((width, tokens), BF16),
            pltpu.VMEM((tokens, 2 * cols), BF16),
            pltpu.VMEM((asked, RINGS, 2, local_len, width), BF16),
            pltpu.VMEM((asked, RINGS, local_len, width), BF16),
            pltpu.VMEM((asked, RINGS, local_len, width), BF16),
            pltpu.VMEM((spans, local_len, width), BF16),
            pltpu.VMEM((spans, local_len, width), BF16),
            pltpu.VMEM((asked, local_len, width), BF16),
            pltpu.VMEM((asked, local_len, width), BF16),
            pltpu.VMEM((2 * width, cols), BF16),
            pltpu.VMEM((places - 1, piece, cols), BF16),
            pltpu.VMEM((2, piece // 2, cols), BF16),
            pltpu.VMEM((piece // 2, cols), BF16),
            pltpu.VMEM((2, piece // 2, cols), BF16),
            pltpu.VMEM((places - 1, 2, piece // 2, cols), BF16),
            dma((spans,)),
            dma((spans,)),
            dma((spans,)),
            dma((spans,)),
            dma((spans,)),
            dma((2, spans)),
            dma((2, spans)),
            dma((4,)),
            dma((17,)),
        ],
        compiler_params=pltpu.CompilerParams(
            collective_id=0, has_side_effects=True, vmem_limit_bytes=58 * 1024 * 1024
        ),
        cost_estimate=pl.CostEstimate(
            flops=14 * 10**9, bytes_accessed=2 * 10**7, transcendentals=720896
        ),
    )(mine_states, queries, grad_attn, enc_gain.reshape(1, width), key_weight, value_weight)


def body(queries, nb_states, nb_owner, nb_row, enc_gain, key_weight, value_weight, grad_attn):
    groups = lax.axis_size("dp")
    owner_list = nb_owner.reshape(-1)
    row_list = nb_row.reshape(-1)
    asked_count = owner_list.shape[0]
    capacity = max(2, (2 * asked_count + groups - 1) // groups)
    positions = jnp.arange(asked_count, dtype=jnp.int32)
    same_owner = owner_list[:, None] == owner_list[None, :]
    before_me = positions[None, :] < positions[:, None]
    slot_rank = jnp.sum(jnp.where(same_owner & before_me, 1, 0), axis=1).astype(jnp.int32)
    slot_index = owner_list * capacity + slot_rank
    slot_count = groups * capacity
    selector = slot_index[:, None] == jnp.arange(slot_count, dtype=jnp.int32)[None, :]
    request = jnp.sum(jnp.where(selector, row_list[:, None], 0), axis=0).reshape(groups, capacity)
    asked_rows = lax.all_to_all(request, "dp", split_axis=0, concat_axis=0, tiled=True)
    asked_flat = asked_rows.reshape(-1)
    local_len = nb_states.shape[1]
    enc_width = nb_states.shape[2]
    outgoing = nb_states[asked_flat].reshape(groups, capacity, local_len, enc_width)
    fetched = lax.all_to_all(outgoing, "dp", split_axis=0, concat_axis=0, tiled=True)
    select_half = selector.astype(jnp.bfloat16)
    mine_states = jnp.dot(
        select_half,
        fetched.reshape(slot_count, local_len * enc_width),
        preferred_element_type=jnp.float32,
    )
    mine_states = mine_states.astype(jnp.bfloat16).reshape(asked_count, local_len, enc_width)
    attn_out, grad_queries, grad_raw, grad_w = layer(
        mine_states,
        queries,
        grad_attn,
        enc_gain,
        key_weight,
        value_weight,
        nb_owner.shape[0],
        groups,
    )
    grad_w = grad_w.reshape(2, enc_width, key_weight.shape[1])
    outgoing_grad = jnp.dot(
        select_half.T,
        grad_raw.reshape(asked_count, local_len * enc_width),
        preferred_element_type=jnp.float32,
    )
    outgoing_grad = outgoing_grad.astype(jnp.bfloat16).reshape(
        groups, capacity, local_len, enc_width
    )
    returned = lax.all_to_all(outgoing_grad, "dp", split_axis=0, concat_axis=0, tiled=True)
    owned_count = nb_states.shape[0]
    owner_rows = (asked_flat[None, :] == jnp.arange(owned_count, dtype=jnp.int32)[:, None]).astype(
        jnp.bfloat16
    )
    grad_states = jnp.dot(
        owner_rows,
        returned.reshape(slot_count, local_len * enc_width),
        preferred_element_type=jnp.float32,
    )
    grad_states = grad_states.astype(jnp.bfloat16).reshape(nb_states.shape)
    return (attn_out, grad_queries, grad_states, grad_w[0], grad_w[1])


def solution(mesh):
    return jax.shard_map(
        body,
        mesh=mesh,
        in_specs=(
            P("dp", "tensor"),
            P("dp", "tensor", None),
            P("dp", None),
            P("dp", None),
            P(),
            P(None, "tensor"),
            P(None, "tensor"),
            P("dp", "tensor"),
        ),
        out_specs=(
            P("dp", "tensor"),
            P("dp", "tensor"),
            P("dp", "tensor", None),
            P(None, "tensor"),
            P(None, "tensor"),
        ),
        check_vma=False,
    )
```

```python
import jax
import jax.numpy as jnp
from jax import lax
from jax.experimental import pallas as pl
from jax.experimental.pallas import tpu as pltpu
from jax.sharding import PartitionSpec as P

HEAD_DIM = 128
MESH = pl.DeviceIdType.MESH
SCALE = HEAD_DIM ** (-0.5)
RINGS = 4
F32 = jnp.float32
BF16 = jnp.bfloat16

epsilon = 1e-06


def normalize(values):
    widened = values.astype(F32)
    inverse = lax.rsqrt(jnp.mean(widened * widened, axis=-1, keepdims=True) + epsilon)
    return (widened * inverse, inverse)


def dot(a, b, ca, cb):
    return lax.dot_general(a, b, (((ca,), (cb,)), ((), ())), preferred_element_type=F32)


def drain(ref, sem):
    pltpu.make_async_copy(ref, ref, sem).wait()


def send(src, dst, send_sem, recv_sem, device):
    pltpu.make_async_remote_copy(
        src_ref=src,
        dst_ref=dst,
        send_sem=send_sem,
        recv_sem=recv_sem,
        device_id=device,
        device_id_type=MESH,
    ).start()


def layer_kernel(
    spans,
    per,
    places,
    slot_of,
    source_of,
    request,
    states,
    queries,
    grads,
    gain,
    key_w,
    value_w,
    attn_out,
    grad_q,
    grad_states,
    grad_key_w,
    grad_value_w,
    asked,
    asked_s,
    stage,
    fetched,
    mine,
    grad_raw,
    returned,
    slot_rows,
    full,
    enc_t,
    grad_kv,
    term,
    from_core,
    sums,
    near_a,
    near_b,
    far_a,
    far_b,
    w_terms,
    w_slots,
    w_half,
    w_other,
    w_mine,
    w_back,
    left_sem,
    right_sem,
    half_sem,
    core_sem,
    swap_sem,
    first_sem,
    second_sem,
    w_sem,
    out_sem,
    near_sem,
):
    me_dp = lax.axis_index("dp")
    me_t = lax.axis_index("tensor")
    ring, core = me_t // 2, lax.rem(me_t, 2)
    place, low = me_dp // 2, lax.rem(me_dp, 2)
    r_ring, l_ring, o_ring = (lax.rem(ring + d, RINGS) for d in (1, 3, 2))
    right = {"tensor": r_ring * 2 + core}
    left = {"tensor": l_ring * 2 + core}
    twin = {"tensor": ring * 2 + 1 - core}
    mate = {"dp": place * 2 + 1 - low}
    groups = 2 * places

    def place_at(k):
        return lax.rem(place + k, places)

    def ahead(k):
        return {"dp": lax.rem(me_dp + k, groups)}

    def behind(k):
        return {"dp": lax.rem(me_dp + groups - k, groups)}

    barrier = pltpu.get_barrier_semaphore()
    for device in (right, left, twin):
        pl.semaphore_signal(barrier, inc=1, device_id=device, device_id_type=MESH)

    def greet(k, carry):
        pl.semaphore_signal(barrier, inc=1, device_id=ahead(k), device_id_type=MESH)
        return carry

    lax.fori_loop(1, groups, greet, 0)
    pl.semaphore_wait(barrier, 3 + groups - 1)

    def ask(k, carry):
        owner = lax.rem(me_dp + k, groups)
        send(request.at[owner], asked.at[k - 1], near_sem.at[0], near_sem.at[1], ahead(k))
        return carry

    lax.fori_loop(1, groups, ask, 0)
    remote_asked = asked.at[pl.ds(0, groups - 1)]
    asked[groups - 1] = request[me_dp]
    drain(remote_asked, near_sem.at[1])
    to_scalars = pltpu.make_async_copy(asked, asked_s, near_sem.at[2])
    to_scalars.start()
    to_scalars.wait()

    def answer(k, carry):
        for r in range(2):
            stage[2 * (k - 1) + r] = states[asked_s[k - 1, 0, r]]
        at = pl.ds(2 * (k - 1), 2)
        send(stage.at[at], fetched.at[at], near_sem.at[3], near_sem.at[4], behind(k))
        return carry

    lax.fori_loop(1, groups, answer, 0)
    for r in range(2):
        fetched[2 * (groups - 1) + r] = states[asked_s[groups - 1, 0, r]]
    others = pl.ds(0, 2 * (groups - 1))
    drain(fetched.at[others], near_sem.at[4])

    gain_row = gain[...]
    span_len = queries.shape[0] // spans
    local_len, width = mine.shape[1], mine.shape[2]
    tokens = per * 2 * RINGS * local_len
    cols = queries.shape[1]

    def rows_of(c):
        return pl.ds(c * per, per)

    def gather_step(i, carry):
        @pl.when(i < spans)
        def _():
            at = rows_of(i)
            for n in range(per):
                mine[i * per + n] = fetched[slot_of[i * per + n]]
            here = full.at[at, ring, core]
            block = mine.at[at]
            send(block, here, out_sem.at[0], left_sem.at[i], right)
            send(block, here, out_sem.at[1], right_sem.at[i], left)
            send(block, here, out_sem.at[2], core_sem.at[i], twin)
            full[at, ring, core] = mine[at]

        j = i - 2

        @pl.when((j >= 0) & (j < spans))
        def _():
            at = rows_of(j)
            from_left = full.at[at, l_ring, core]
            from_right = full.at[at, r_ring, core]
            drain(from_left, left_sem.at[j])
            one = full.at[j * per, l_ring, core]
            send(one, one, out_sem.at[3], half_sem.at[j], right)
            send(from_left, from_left, out_sem.at[5], core_sem.at[j], twin)
            drain(from_right, right_sem.at[j])
            two = full.at[j * per + 1, r_ring, core]
            send(two, two, out_sem.at[4], half_sem.at[j], left)
            send(from_right, from_right, out_sem.at[6], core_sem.at[j], twin)

        k = i - 4

        @pl.when((k >= 0) & (k < spans))
        def _():
            across = full.at[rows_of(k), o_ring, core]
            drain(across, half_sem.at[k])
            send(across, across, out_sem.at[7], core_sem.at[k], twin)

        c = i - 5

        @pl.when(c >= 0)
        def _():
            at = rows_of(c)
            drain(full.at[at, :, 1 - core], core_sem.at[c])
            unit, _ = normalize(full[at].reshape(tokens, width))
            encoded = (unit * gain_row).astype(BF16)
            enc_t[:, pl.ds(pl.multiple_of(c * tokens, tokens), tokens)] = encoded.T
            keys = dot(encoded, key_w[...], 1, 0).astype(BF16)
            values = dot(encoded, value_w[...], 1, 0).astype(BF16)
            q_rows = pl.ds(pl.multiple_of(c * span_len, span_len), span_len)
            t_rows = pl.ds(pl.multiple_of(c * tokens, tokens), tokens)
            for h in range(cols // HEAD_DIM):
                lanes = slice(h * HEAD_DIM, (h + 1) * HEAD_DIM)
                q, g = queries[q_rows, lanes], grads[q_rows, lanes]
                kh, vh = keys[:, lanes], values[:, lanes]
                exponent = jnp.exp(dot(q, kh, 1, 1) * SCALE)
                p = exponent / jnp.sum(exponent, axis=-1, keepdims=True)
                w = p.astype(BF16)
                attn_out[q_rows, lanes] = dot(w, vh, 1, 0).astype(BF16)
                gw = dot(g, vh, 1, 1)
                gs = (p * (gw - jnp.sum(p * gw, axis=-1, keepdims=True)) * SCALE).astype(BF16)
                grad_q[q_rows, lanes] = dot(gs, kh, 1, 0).astype(BF16)
                grad_kv[t_rows, lanes] = dot(gs, q, 0, 0).astype(BF16)
                v_lanes = slice(cols + h * HEAD_DIM, cols + (h + 1) * HEAD_DIM)
                grad_kv[t_rows, v_lanes] = dot(w, g, 0, 0).astype(BF16)

        return carry

    lax.fori_loop(0, spans + 5, gather_step, 0)

    tile = 256
    tiles = width // tile

    def weight_tile(n):
        part = n // tiles
        r = lax.rem(n, tiles)
        left_side = enc_t[pl.ds(pl.multiple_of(r * tile, tile), tile), :]
        lanes = pl.ds(pl.multiple_of(part * cols, cols), cols)
        row = pl.multiple_of(n * tile, tile)
        w_terms[pl.ds(row, tile), :] = dot(left_side, grad_kv[:, lanes], 1, 0).astype(BF16)

    piece = w_slots.shape[1]
    half = piece // 2

    def piece_rows(p):
        return pl.ds(pl.multiple_of(p * piece, piece), piece)

    def scatter(k, carry):
        p = place_at(k)
        send(
            w_terms.at[piece_rows(p)],
            w_slots.at[k - 1],
            out_sem.at[8],
            w_sem.at[0],
            {"dp": p * 2 + low},
        )
        return carry

    def reduce_step(i, carry):
        @pl.when(i < spans)
        def _():
            t_rows = pl.ds(pl.multiple_of(i * tokens, tokens), tokens)
            product = dot(grad_kv[t_rows, :cols], key_w[...], 1, 1)
            product = product + dot(grad_kv[t_rows, cols:], value_w[...], 1, 1)
            at = rows_of(i)
            term[at] = product.astype(BF16).reshape(per, RINGS, 2, local_len, width)
            send(
                term.at[at, :, 1 - core],
                from_core.at[at],
                out_sem.at[9],
                swap_sem.at[i],
                twin,
            )

        j = i - 1

        @pl.when((j >= 0) & (j < spans))
        def _():
            at = rows_of(j)
            drain(from_core.at[at], swap_sem.at[j])
            total = term[at, :, core].astype(F32) + from_core[at].astype(F32)
            sums[at] = total.astype(BF16)
            send(sums.at[j * per, o_ring], near_a.at[j], out_sem.at[10], first_sem.at[0, j], right)
            send(
                sums.at[j * per + 1, o_ring], near_b.at[j], out_sem.at[11], first_sem.at[1, j], left
            )

        k = i - 3

        @pl.when((k >= 0) & (k < spans))
        def _():
            at = rows_of(k)
            drain(near_a.at[k], first_sem.at[0, k])
            total = sums[k * per, r_ring].astype(F32) + near_a[k].astype(F32)
            sums[k * per, r_ring] = total.astype(BF16)
            send(sums.at[at, r_ring], far_a.at[at], out_sem.at[12], second_sem.at[0, k], right)
            drain(near_b.at[k], first_sem.at[1, k])
            total = sums[k * per + 1, l_ring].astype(F32) + near_b[k].astype(F32)
            sums[k * per + 1, l_ring] = total.astype(BF16)
            send(sums.at[at, l_ring], far_b.at[at], out_sem.at[13], second_sem.at[1, k], left)

        @pl.when(i < 3)
        def _():
            def tile_step(n, carry):
                weight_tile(2 * i + n)
                return carry

            lax.fori_loop(0, 2, tile_step, 0)

        @pl.when(i == 2)
        def _():
            lax.fori_loop(1, places, scatter, 0)

        @pl.when(i == 8)
        def _():
            drain(w_slots, w_sem.at[0])
            total = w_terms[piece_rows(place), :].astype(F32)
            for s in range(places - 1):
                total = total + w_slots[s].astype(F32)
            w_half[...] = total.astype(BF16).reshape(2, half, cols)
            send(w_half.at[1 - low], w_other, out_sem.at[14], w_sem.at[1], mate)

        @pl.when(i == 9)
        def _():
            drain(w_other, w_sem.at[1])
            total = w_half[low].astype(F32) + w_other[...].astype(F32)
            w_mine[low] = total.astype(BF16)
            send(w_mine.at[low], w_mine.at[low], out_sem.at[15], w_sem.at[2], mate)

        @pl.when(i == 10)
        def _():
            drain(w_mine.at[1 - low], w_sem.at[2])

            def spread(k, carry):
                device = {"dp": place_at(k) * 2 + low}
                send(w_mine, w_back.at[k - 1], out_sem.at[16], w_sem.at[3], device)
                return carry

            lax.fori_loop(1, places, spread, 0)

        c = i - 5

        @pl.when(c >= 0)
        def _():
            at = rows_of(c)
            drain(far_a.at[at], second_sem.at[0, c])
            drain(far_b.at[at], second_sem.at[1, c])
            own = sums[at, ring].astype(F32) + far_a[at].astype(F32) + far_b[at].astype(F32)
            own = own.reshape(per * local_len, width)
            unit, inverse = normalize(mine[at].reshape(per * local_len, width))
            scaled = own * gain_row
            raw = inverse * (scaled - unit * jnp.mean(scaled * unit, axis=-1, keepdims=True))
            grad_raw[at] = raw.astype(BF16).reshape(per, local_len, width)

        return carry

    lax.fori_loop(0, spans + 5, reduce_step, 0)

    asked_count = spans * per
    grad_raw[asked_count] = jnp.zeros((local_len, width), BF16)
    drain(stage.at[others], near_sem.at[3])

    def give_back(k, carry):
        for r in range(2):
            stage[2 * (k - 1) + r] = grad_raw[source_of[2 * (k - 1) + r]]
        at = pl.ds(2 * (k - 1), 2)
        send(stage.at[at], returned.at[at], near_sem.at[5], near_sem.at[6], ahead(k))
        return carry

    lax.fori_loop(1, groups, give_back, 0)
    for r in range(2):
        returned[2 * (groups - 1) + r] = grad_raw[source_of[2 * (groups - 1) + r]]

    def name_rows(k, carry):
        for r in range(2):
            rows = pl.ds(pl.multiple_of((2 * k + r) * local_len, local_len), local_len)
            slot_rows[rows, :] = jnp.full((local_len, 256), asked_s[k, 0, r], jnp.int32)
        return carry

    lax.fori_loop(0, groups, name_rows, 0)

    drain(w_back, w_sem.at[3])

    def keep(source, value):
        @pl.when(source < places // 2)
        def _():
            grad_key_w[source] = value

        @pl.when(source >= places // 2)
        def _():
            grad_value_w[source - places // 2] = value

    keep(place, w_mine[...])

    def settle(k, carry):
        keep(lax.rem(place + places - k, places), w_back[k - 1])
        return carry

    lax.fori_loop(1, places, settle, 0)

    slot_tokens = 2 * groups * local_len
    owned = states.shape[0] * local_len
    shape = (slot_tokens, owned)
    to_row = lax.broadcasted_iota(jnp.int32, shape, 1)
    token = lax.broadcasted_iota(jnp.int32, shape, 0)
    wanted = slot_rows[...] * local_len + lax.rem(token, local_len)
    chosen = jnp.where(wanted == to_row, 1.0, 0.0).astype(BF16)
    drain(returned.at[others], near_sem.at[6])
    total = dot(chosen, returned[...].reshape(slot_tokens, width), 0, 0)
    grad_states[...] = total.astype(BF16).reshape(states.shape)

    drain(remote_asked, near_sem.at[0])
    drain(stage.at[others], near_sem.at[5])
    for n in (0, 1, 2, 5, 6, 7):
        drain(mine, out_sem.at[n])
    drain(near_a, out_sem.at[3])
    drain(near_a, out_sem.at[4])
    drain(w_slots, out_sem.at[8])
    drain(from_core, out_sem.at[9])
    drain(near_a, out_sem.at[10])
    drain(near_b, out_sem.at[11])
    drain(far_a, out_sem.at[12])
    drain(far_b, out_sem.at[13])
    drain(w_other, out_sem.at[14])
    drain(w_other, out_sem.at[15])
    drain(w_back, out_sem.at[16])


def layer(
    slot_of, source_of, request, states, queries, grad_attn, enc_gain, key_weight, value_weight
):
    groups = request.shape[0]
    owned, local_len, width = states.shape
    asked = slot_of.shape[0]
    per = 2
    spans = asked // per
    rows, cols = queries.shape
    places = groups // 2
    tokens = asked * local_len * RINGS * 2
    piece = 2 * width // places

    def kernel(*refs):
        layer_kernel(spans, per, places, *refs)

    vmem = pl.BlockSpec(memory_space=pltpu.VMEM)
    smem = pl.BlockSpec(memory_space=pltpu.SMEM)
    dma = pltpu.SemaphoreType.DMA
    return pl.pallas_call(
        kernel,
        out_shape=(
            jax.ShapeDtypeStruct((rows, cols), BF16),
            jax.ShapeDtypeStruct((rows, cols), BF16),
            jax.ShapeDtypeStruct((owned, local_len, width), BF16),
            jax.ShapeDtypeStruct((places // 2, 2, piece // 2, cols), BF16),
            jax.ShapeDtypeStruct((places // 2, 2, piece // 2, cols), BF16),
        ),
        in_specs=[smem] * 2 + [vmem] * 7,
        out_specs=(vmem,) * 5,
        scratch_shapes=[
            pltpu.VMEM((groups, 1, 128), jnp.int32),
            pltpu.SMEM((groups, 1, 128), jnp.int32),
            pltpu.VMEM((2 * groups, local_len, width), BF16),
            pltpu.VMEM((2 * groups, local_len, width), BF16),
            pltpu.VMEM((asked, local_len, width), BF16),
            pltpu.VMEM((asked + 1, local_len, width), BF16),
            pltpu.VMEM((2 * groups, local_len, width), BF16),
            pltpu.VMEM((2 * groups * local_len, owned * local_len), jnp.int32),
            pltpu.VMEM((asked, RINGS, 2, local_len, width), BF16),
            pltpu.VMEM((width, tokens), BF16),
            pltpu.VMEM((tokens, 2 * cols), BF16),
            pltpu.VMEM((asked, RINGS, 2, local_len, width), BF16),
            pltpu.VMEM((asked, RINGS, local_len, width), BF16),
            pltpu.VMEM((asked, RINGS, local_len, width), BF16),
            pltpu.VMEM((spans, local_len, width), BF16),
            pltpu.VMEM((spans, local_len, width), BF16),
            pltpu.VMEM((asked, local_len, width), BF16),
            pltpu.VMEM((asked, local_len, width), BF16),
            pltpu.VMEM((2 * width, cols), BF16),
            pltpu.VMEM((places - 1, piece, cols), BF16),
            pltpu.VMEM((2, piece // 2, cols), BF16),
            pltpu.VMEM((piece // 2, cols), BF16),
            pltpu.VMEM((2, piece // 2, cols), BF16),
            pltpu.VMEM((places - 1, 2, piece // 2, cols), BF16),
            dma((spans,)),
            dma((spans,)),
            dma((spans,)),
            dma((spans,)),
            dma((spans,)),
            dma((2, spans)),
            dma((2, spans)),
            dma((4,)),
            dma((17,)),
            dma((7,)),
        ],
        compiler_params=pltpu.CompilerParams(
            collective_id=0, has_side_effects=True, vmem_limit_bytes=58 * 1024 * 1024
        ),
        cost_estimate=pl.CostEstimate(
            flops=14 * 10**9, bytes_accessed=2 * 10**7, transcendentals=720896
        ),
    )(
        slot_of,
        source_of,
        request,
        states,
        queries,
        grad_attn,
        enc_gain.reshape(1, width),
        key_weight,
        value_weight,
    )


def body(queries, nb_states, nb_owner, nb_row, enc_gain, key_weight, value_weight, grad_attn):
    groups = lax.axis_size("dp")
    owner_list = nb_owner.reshape(-1)
    row_list = nb_row.reshape(-1)
    asked_count = owner_list.shape[0]
    capacity = 2
    positions = jnp.arange(asked_count, dtype=jnp.int32)
    same_owner = owner_list[:, None] == owner_list[None, :]
    before_me = positions[None, :] < positions[:, None]
    slot_rank = jnp.sum(jnp.where(same_owner & before_me, 1, 0), axis=1).astype(jnp.int32)
    me = lax.axis_index("dp")
    slot_of = lax.rem(owner_list - me - 1 + groups, groups) * capacity + slot_rank
    slot_count = groups * capacity
    slots = jnp.arange(slot_count, dtype=jnp.int32)
    filled = slot_of[:, None] == slots[None, :]
    source_of = asked_count - jnp.sum(
        jnp.where(filled, asked_count - positions[:, None], 0), axis=0
    ).astype(jnp.int32)
    owner_rank = owner_list * capacity + slot_rank
    named = owner_rank[:, None] == slots[None, :]
    request = jnp.sum(jnp.where(named, row_list[:, None], 0), axis=0).astype(jnp.int32)
    request = jnp.pad(request.reshape(groups, 1, capacity), ((0, 0), (0, 0), (0, 128 - capacity)))
    attn_out, grad_queries, grad_states, grad_key_w, grad_value_w = layer(
        slot_of,
        source_of,
        request,
        nb_states,
        queries,
        grad_attn,
        enc_gain,
        key_weight,
        value_weight,
    )
    grad_key_w = grad_key_w.astype(F32).reshape(key_weight.shape)
    grad_value_w = grad_value_w.astype(F32).reshape(value_weight.shape)
    return (attn_out, grad_queries, grad_states, grad_key_w, grad_value_w)


def solution(mesh):
    return jax.shard_map(
        body,
        mesh=mesh,
        in_specs=(
            P("dp", "tensor"),
            P("dp", "tensor", None),
            P("dp", None),
            P("dp", None),
            P(),
            P(None, "tensor"),
            P(None, "tensor"),
            P("dp", "tensor"),
        ),
        out_specs=(
            P("dp", "tensor"),
            P("dp", "tensor"),
            P("dp", "tensor", None),
            P(None, "tensor"),
            P(None, "tensor"),
        ),
        check_vma=False,
    )
```

```python
import jax
import jax.numpy as jnp
from jax import lax
from jax.experimental import pallas as pl
from jax.experimental.pallas import tpu as pltpu
from jax.sharding import PartitionSpec as P

HEAD_DIM = 128
MESH = pl.DeviceIdType.MESH
SCALE = HEAD_DIM ** (-0.5)
RINGS = 4
F32 = jnp.float32
BF16 = jnp.bfloat16

epsilon = 1e-06


def normalize(values):
    widened = values.astype(F32)
    inverse = lax.rsqrt(jnp.mean(widened * widened, axis=-1, keepdims=True) + epsilon)
    return (widened * inverse, inverse)


def dot(a, b, ca, cb):
    return lax.dot_general(a, b, (((ca,), (cb,)), ((), ())), preferred_element_type=F32)


def drain(ref, sem):
    pltpu.make_async_copy(ref, ref, sem).wait()


def send(src, dst, send_sem, recv_sem, device):
    pltpu.make_async_remote_copy(
        src_ref=src,
        dst_ref=dst,
        send_sem=send_sem,
        recv_sem=recv_sem,
        device_id=device,
        device_id_type=MESH,
    ).start()


def layer_kernel(
    spans,
    per,
    places,
    slot_of,
    source_of,
    request,
    gain,
    states_hbm,
    queries_hbm,
    grads_hbm,
    key_w_hbm,
    value_w_hbm,
    grad_states,
    attn_hbm,
    grad_q_hbm,
    grad_key_w_hbm,
    grad_value_w_hbm,
    states,
    queries,
    grads,
    key_w,
    value_w,
    attn_out,
    grad_q,
    grad_key_w,
    grad_value_w,
    asked,
    asked_s,
    stage,
    fetched,
    mine,
    back,
    grad_raw,
    returned,
    slot_rows,
    full,
    enc_t,
    grad_kv,
    term,
    from_core,
    sums,
    near_a,
    near_b,
    far_a,
    far_b,
    w_terms,
    w_big,
    w_mid,
    w_small,
    w_piece,
    w_other,
    w_done,
    w_near,
    w_quarter,
    w_far,
    left_sem,
    right_sem,
    half_sem,
    core_sem,
    swap_sem,
    first_sem,
    second_sem,
    w_sem,
    out_sem,
    swap_out,
    w_out,
    near_sem,
    local_sem,
):
    me_dp = lax.axis_index("dp")
    me_t = lax.axis_index("tensor")
    ring, core = me_t // 2, lax.rem(me_t, 2)
    place, low = me_dp // 2, lax.rem(me_dp, 2)
    r_ring, l_ring, o_ring = (lax.rem(ring + d, RINGS) for d in (1, 3, 2))
    right = {"tensor": r_ring * 2 + core}
    left = {"tensor": l_ring * 2 + core}
    twin = {"tensor": ring * 2 + 1 - core}
    mate = {"dp": place * 2 + 1 - low}
    groups = 2 * places

    y, x = place // 4, lax.rem(place, 4)

    first_at, second_at = (x, y), (y, x)

    def along(axis, d):
        if axis == 0:
            return {"dp": (y * 4 + lax.rem(x + d, 4)) * 2 + low}
        return {"dp": (lax.rem(y + d, 4) * 4 + x) * 2 + low}

    loads = [
        pltpu.make_async_copy(src, dst, local_sem.at[n])
        for n, (src, dst) in enumerate(
            (
                (states_hbm, states),
                (queries_hbm, queries),
                (grads_hbm, grads),
                (key_w_hbm, key_w),
                (value_w_hbm, value_w),
            )
        )
    ]
    stores = [
        pltpu.make_async_copy(src, dst, local_sem.at[5 + n])
        for n, (src, dst) in enumerate(
            (
                (attn_out, attn_hbm),
                (grad_q, grad_q_hbm),
                (grad_key_w, grad_key_w_hbm),
                (grad_value_w, grad_value_w_hbm),
            )
        )
    ]
    for load in loads:
        load.start()

    def ahead(k):
        return {"dp": lax.rem(me_dp + k, groups)}

    def behind(k):
        return {"dp": lax.rem(me_dp + groups - k, groups)}

    barrier = pltpu.get_barrier_semaphore()
    for device in (right, left, twin):
        pl.semaphore_signal(barrier, inc=1, device_id=device, device_id_type=MESH)

    def greet(k, carry):
        pl.semaphore_signal(barrier, inc=1, device_id=ahead(k), device_id_type=MESH)
        return carry

    lax.fori_loop(1, groups, greet, 0)
    pl.semaphore_wait(barrier, 3 + groups - 1)

    def ask(k, carry):
        owner = lax.rem(me_dp + k, groups)
        send(request.at[owner], asked.at[k - 1], near_sem.at[0], near_sem.at[1], ahead(k))
        return carry

    lax.fori_loop(1, groups, ask, 0)
    remote_asked = asked.at[pl.ds(0, groups - 1)]
    asked[groups - 1] = request[me_dp]
    drain(remote_asked, near_sem.at[1])
    to_scalars = pltpu.make_async_copy(asked, asked_s, near_sem.at[2])
    to_scalars.start()
    to_scalars.wait()

    width = states.shape[2]
    others = pl.ds(0, 2 * (groups - 1))
    loads[0].wait()

    def answer(k, carry):
        for r in range(2):
            stage[2 * (k - 1) + r] = states[asked_s[k - 1, 0, r]]
        at = pl.ds(2 * (k - 1), 2)
        send(stage.at[at], fetched.at[at], near_sem.at[3], near_sem.at[4], behind(k))
        return carry

    lax.fori_loop(1, groups, answer, 0)
    for r in range(2):
        fetched[2 * (groups - 1) + r] = states[asked_s[groups - 1, 0, r]]
    for load in loads[1:]:
        load.wait()
    drain(fetched.at[others], near_sem.at[4])

    gain_row = gain[...].reshape(1, width)
    span_len = queries.shape[0] // spans
    local_len = states.shape[1]
    tokens = per * 2 * RINGS * local_len
    cols = queries.shape[1]

    def rows_of(c):
        return pl.ds(c * per, per)

    def gather_step(i, carry):
        @pl.when(i < spans)
        def _():
            at = rows_of(i)
            for n in range(per):
                mine[i * per + n] = fetched[slot_of[i * per + n]]
            here = full.at[at, ring, core]
            block = mine.at[at]
            send(block, here, out_sem.at[0], left_sem.at[i], right)
            send(block, here, out_sem.at[1], right_sem.at[i], left)
            send(block, here, out_sem.at[2], core_sem.at[i], twin)
            full[at, ring, core] = mine[at]

        j = i - 2

        @pl.when((j >= 0) & (j < spans))
        def _():
            at = rows_of(j)
            from_left = full.at[at, l_ring, core]
            from_right = full.at[at, r_ring, core]
            drain(from_left, left_sem.at[j])
            one = full.at[j * per, l_ring, core]
            send(one, one, out_sem.at[3], half_sem.at[j], right)
            drain(from_right, right_sem.at[j])
            two = full.at[j * per + 1, r_ring, core]
            send(two, two, out_sem.at[4], half_sem.at[j], left)
            send(from_left, from_left, out_sem.at[5], core_sem.at[j], twin)
            send(from_right, from_right, out_sem.at[6], core_sem.at[j], twin)

        k = i - 4

        @pl.when((k >= 0) & (k < spans))
        def _():
            across = full.at[rows_of(k), o_ring, core]
            drain(across, half_sem.at[k])
            send(across, across, out_sem.at[7], core_sem.at[k], twin)

        c = i - 5

        @pl.when(c >= 0)
        def _():
            at = rows_of(c)
            drain(full.at[at, :, 1 - core], core_sem.at[c])
            raw = full[at].reshape(tokens, width)
            unit, _ = normalize(raw)
            encoded = (unit * gain_row).astype(BF16)
            enc_t[:, pl.ds(pl.multiple_of(c * tokens, tokens), tokens)] = encoded.T
            keys = dot(encoded, key_w[...], 1, 0).astype(BF16)
            values = dot(encoded, value_w[...], 1, 0).astype(BF16)
            q_rows = pl.ds(pl.multiple_of(c * span_len, span_len), span_len)
            t_rows = pl.ds(pl.multiple_of(c * tokens, tokens), tokens)
            for h in range(cols // HEAD_DIM):
                lanes = slice(h * HEAD_DIM, (h + 1) * HEAD_DIM)
                q, g = queries[q_rows, lanes], grads[q_rows, lanes]
                kh, vh = keys[:, lanes], values[:, lanes]
                exponent = jnp.exp(dot(q, kh, 1, 1) * SCALE)
                p = exponent / jnp.sum(exponent, axis=-1, keepdims=True)
                w = p.astype(BF16)
                attn_out[q_rows, lanes] = dot(w, vh, 1, 0).astype(BF16)
                gw = dot(g, vh, 1, 1)
                gs = (p * (gw - jnp.sum(p * gw, axis=-1, keepdims=True)) * SCALE).astype(BF16)
                grad_q[q_rows, lanes] = dot(gs, kh, 1, 0).astype(BF16)
                grad_kv[t_rows, lanes] = dot(gs, q, 0, 0).astype(BF16)
                v_lanes = slice(cols + h * HEAD_DIM, cols + (h + 1) * HEAD_DIM)
                grad_kv[t_rows, v_lanes] = dot(w, g, 0, 0).astype(BF16)

        return carry

    lax.fori_loop(0, spans + 5, gather_step, 0)
    stores[0].start()
    stores[1].start()

    tile = 256
    tiles = width // tile

    def weight_tile(n):
        part = n // tiles
        r = lax.rem(n, tiles)
        left_side = enc_t[pl.ds(pl.multiple_of(r * tile, tile), tile), :]
        lanes = pl.ds(pl.multiple_of(part * cols, cols), cols)
        row = pl.multiple_of(n * tile, tile)
        w_terms[pl.ds(row, tile), :] = dot(left_side, grad_kv[:, lanes], 1, 0).astype(BF16)

    quarter = width // 4
    piece = quarter // 4

    def quarter_rows(part, a):
        return pl.ds(pl.multiple_of(part * width + a * quarter, quarter), quarter)

    def reduce_step(i, carry):
        @pl.when(i < spans)
        def _():
            t_rows = pl.ds(pl.multiple_of(i * tokens, tokens), tokens)
            product = dot(grad_kv[t_rows, :cols], key_w[...], 1, 1)
            product = product + dot(grad_kv[t_rows, cols:], value_w[...], 1, 1)
            at = rows_of(i)
            term[at] = product.astype(BF16).reshape(per, RINGS, 2, local_len, width)
            send(
                term.at[at, :, 1 - core],
                from_core.at[at],
                swap_out.at[0],
                swap_sem.at[i],
                twin,
            )

        j = i - 1

        @pl.when((j >= 0) & (j < spans))
        def _():
            at = rows_of(j)
            drain(from_core.at[at], swap_sem.at[j])
            total = term[at, :, core].astype(F32) + from_core[at].astype(F32)
            sums[at] = total.astype(BF16)
            send(sums.at[j * per, o_ring], near_a.at[j], swap_out.at[1], first_sem.at[0, j], right)
            send(
                sums.at[j * per + 1, o_ring], near_b.at[j], swap_out.at[2], first_sem.at[1, j], left
            )

        k = i - 3

        @pl.when((k >= 0) & (k < spans))
        def _():
            at = rows_of(k)
            drain(near_a.at[k], first_sem.at[0, k])
            total = sums[k * per, r_ring].astype(F32) + near_a[k].astype(F32)
            sums[k * per, r_ring] = total.astype(BF16)
            send(sums.at[at, r_ring], far_a.at[at], swap_out.at[3], second_sem.at[0, k], right)
            drain(near_b.at[k], first_sem.at[1, k])
            total = sums[k * per + 1, l_ring].astype(F32) + near_b[k].astype(F32)
            sums[k * per + 1, l_ring] = total.astype(BF16)
            send(sums.at[at, l_ring], far_b.at[at], swap_out.at[4], second_sem.at[1, k], left)

        @pl.when((i == 2) | (i == 3))
        def _():
            def tile_step(n, carry):
                weight_tile(tiles * (i - 2) + n)
                return carry

            lax.fori_loop(0, tiles, tile_step, 0)

        @pl.when(i == 3)
        def _():
            for d in (1, 2, 3):
                for part in range(2):
                    send(
                        w_terms.at[quarter_rows(part, lax.rem(first_at[part] + d, 4))],
                        w_big.at[part, d - 1],
                        w_out.at[0],
                        w_sem.at[0],
                        along(part, d),
                    )

        @pl.when(i == 7)
        def _():
            drain(w_big, w_sem.at[0])
            for part in range(2):
                total = w_terms[quarter_rows(part, first_at[part]), :].astype(F32)
                for d in range(3):
                    total = total + w_big[part, d].astype(F32)
                w_mid[part] = total.astype(BF16).reshape(4, piece, cols)
                for d in (1, 2, 3):
                    send(
                        w_mid.at[part, lax.rem(second_at[part] + d, 4)],
                        w_small.at[part, d - 1],
                        w_out.at[1],
                        w_sem.at[1],
                        along(1 - part, d),
                    )

        @pl.when(i == 8)
        def _():
            drain(w_small, w_sem.at[1])
            for part in range(2):
                total = w_mid[part, second_at[part]].astype(F32)
                for d in range(3):
                    total = total + w_small[part, d].astype(F32)
                w_piece[part] = total.astype(BF16)
            send(w_piece, w_other, w_out.at[2], w_sem.at[2], mate)

        @pl.when(i == 9)
        def _():
            drain(w_other, w_sem.at[2])
            for part in range(2):
                total = w_piece[part].astype(F32) + w_other[part].astype(F32)
                w_done[part] = total.astype(BF16)
                w_quarter[part, second_at[part]] = total.astype(BF16)
                for d in (1, 2, 3):
                    send(
                        w_done.at[part],
                        w_near.at[part, d - 1],
                        w_out.at[3],
                        w_sem.at[3],
                        along(1 - part, d),
                    )

        @pl.when(i == 10)
        def _():
            drain(w_near, w_sem.at[3])
            for part in range(2):
                for d in (1, 2, 3):
                    w_quarter[part, lax.rem(second_at[part] + 4 - d, 4)] = w_near[part, d - 1]
                for d in (1, 2, 3):
                    send(
                        w_quarter.at[part],
                        w_far.at[part, d - 1],
                        w_out.at[4],
                        w_sem.at[4],
                        along(part, d),
                    )

        c = i - 5

        @pl.when(c >= 0)
        def _():
            at = rows_of(c)
            drain(far_a.at[at], second_sem.at[0, c])
            drain(far_b.at[at], second_sem.at[1, c])
            own = sums[at, ring].astype(F32) + far_a[at].astype(F32) + far_b[at].astype(F32)
            own = own.reshape(per * local_len, width)
            unit, inverse = normalize(mine[at].reshape(per * local_len, width))
            scaled = own * gain_row
            raw = inverse * (scaled - unit * jnp.mean(scaled * unit, axis=-1, keepdims=True))
            grad_raw[at] = raw.astype(BF16).reshape(per, local_len, width)

        return carry

    lax.fori_loop(0, spans + 5, reduce_step, 0)

    asked_count = spans * per
    grad_raw[asked_count] = jnp.zeros((local_len, width), BF16)

    def give_back(k, carry):
        for r in range(2):
            back[2 * (k - 1) + r] = grad_raw[source_of[2 * (k - 1) + r]]
        at = pl.ds(2 * (k - 1), 2)
        send(back.at[at], returned.at[at], near_sem.at[5], near_sem.at[6], ahead(k))
        return carry

    lax.fori_loop(1, groups, give_back, 0)
    for r in range(2):
        returned[2 * (groups - 1) + r] = grad_raw[source_of[2 * (groups - 1) + r]]

    def name_rows(k, carry):
        for r in range(2):
            rows = pl.ds(pl.multiple_of((2 * k + r) * local_len, local_len), local_len)
            slot_rows[rows, :] = jnp.full((local_len, 256), asked_s[k, 0, r], jnp.int32)
        return carry

    lax.fori_loop(0, groups, name_rows, 0)

    drain(w_far, w_sem.at[4])
    for part, out in enumerate((grad_key_w, grad_value_w)):
        out[first_at[part]] = w_quarter[part].reshape(quarter, cols).astype(F32)
        for d in (1, 2, 3):
            value = w_far[part, d - 1].reshape(quarter, cols).astype(F32)
            out[lax.rem(first_at[part] + 4 - d, 4)] = value
        stores[2 + part].start()

    slot_tokens = 2 * groups * local_len
    owned = states.shape[0] * local_len
    shape = (slot_tokens, owned)
    to_row = lax.broadcasted_iota(jnp.int32, shape, 1)
    token = lax.broadcasted_iota(jnp.int32, shape, 0)
    wanted = slot_rows[...] * local_len + lax.rem(token, local_len)
    chosen = jnp.where(wanted == to_row, 1.0, 0.0).astype(BF16)
    drain(returned.at[others], near_sem.at[6])
    total = dot(chosen, returned[...].reshape(slot_tokens, width), 0, 0)
    grad_states[...] = total.astype(BF16).reshape(states.shape)

    drain(remote_asked, near_sem.at[0])
    drain(stage.at[others], near_sem.at[3])
    drain(back.at[others], near_sem.at[5])
    few = mine.at[pl.ds(0, spans)]
    for n in (0, 1, 2, 5, 6, 7):
        drain(mine, out_sem.at[n])
    drain(few, out_sem.at[3])
    drain(few, out_sem.at[4])
    drain(from_core, swap_out.at[0])
    drain(near_a, swap_out.at[1])
    drain(near_b, swap_out.at[2])
    drain(far_a, swap_out.at[3])
    drain(far_b, swap_out.at[4])
    for n, ref in enumerate((w_big, w_small, w_other, w_near, w_far)):
        drain(ref, w_out.at[n])
    for store in stores:
        store.wait()


def layer(
    slot_of, source_of, request, states, queries, grad_attn, enc_gain, key_weight, value_weight
):
    groups = request.shape[0]
    owned, local_len, width = states.shape
    asked = slot_of.shape[0]
    per = 2
    spans = asked // per
    rows, cols = queries.shape
    places = groups // 2
    tokens = asked * local_len * RINGS * 2
    quarter, piece = width // 4, width // 16

    def kernel(*refs):
        layer_kernel(spans, per, places, *refs)

    vmem = pl.BlockSpec(memory_space=pltpu.VMEM)
    smem = pl.BlockSpec(memory_space=pltpu.SMEM)
    anywhere = pl.BlockSpec(memory_space=pl.ANY)
    dma = pltpu.SemaphoreType.DMA
    return pl.pallas_call(
        kernel,
        out_shape=(
            jax.ShapeDtypeStruct((owned, local_len, width), BF16),
            jax.ShapeDtypeStruct((rows, cols), BF16),
            jax.ShapeDtypeStruct((rows, cols), BF16),
            jax.ShapeDtypeStruct((4, quarter, cols), F32),
            jax.ShapeDtypeStruct((4, quarter, cols), F32),
        ),
        in_specs=[smem] * 2 + [vmem] * 2 + [anywhere] * 5,
        out_specs=(vmem,) + (anywhere,) * 4,
        scratch_shapes=[
            pltpu.VMEM((owned, local_len, width), BF16),
            pltpu.VMEM((rows, cols), BF16),
            pltpu.VMEM((rows, cols), BF16),
            pltpu.VMEM((width, cols), BF16),
            pltpu.VMEM((width, cols), BF16),
            pltpu.VMEM((rows, cols), BF16),
            pltpu.VMEM((rows, cols), BF16),
            pltpu.VMEM((4, quarter, cols), F32),
            pltpu.VMEM((4, quarter, cols), F32),
            pltpu.VMEM((groups, 1, 128), jnp.int32),
            pltpu.SMEM((groups, 1, 128), jnp.int32),
            pltpu.VMEM((2 * groups, local_len, width), BF16),
            pltpu.VMEM((2 * groups, local_len, width), BF16),
            pltpu.VMEM((asked, local_len, width), BF16),
            pltpu.VMEM((2 * groups, local_len, width), BF16),
            pltpu.VMEM((asked + 1, local_len, width), BF16),
            pltpu.VMEM((2 * groups, local_len, width), BF16),
            pltpu.VMEM((2 * groups * local_len, owned * local_len), jnp.int32),
            pltpu.VMEM((asked, RINGS, 2, local_len, width), BF16),
            pltpu.VMEM((width, tokens), BF16),
            pltpu.VMEM((tokens, 2 * cols), BF16),
            pltpu.VMEM((asked, RINGS, 2, local_len, width), BF16),
            pltpu.VMEM((asked, RINGS, local_len, width), BF16),
            pltpu.VMEM((asked, RINGS, local_len, width), BF16),
            pltpu.VMEM((spans, local_len, width), BF16),
            pltpu.VMEM((spans, local_len, width), BF16),
            pltpu.VMEM((asked, local_len, width), BF16),
            pltpu.VMEM((asked, local_len, width), BF16),
            pltpu.VMEM((2 * width, cols), BF16),
            pltpu.VMEM((2, 3, quarter, cols), BF16),
            pltpu.VMEM((2, 4, piece, cols), BF16),
            pltpu.VMEM((2, 3, piece, cols), BF16),
            pltpu.VMEM((2, piece, cols), BF16),
            pltpu.VMEM((2, piece, cols), BF16),
            pltpu.VMEM((2, piece, cols), BF16),
            pltpu.VMEM((2, 3, piece, cols), BF16),
            pltpu.VMEM((2, 4, piece, cols), BF16),
            pltpu.VMEM((2, 3, 4, piece, cols), BF16),
            dma((spans,)),
            dma((spans,)),
            dma((spans,)),
            dma((spans,)),
            dma((spans,)),
            dma((2, spans)),
            dma((2, spans)),
            dma((5,)),
            dma((8,)),
            dma((5,)),
            dma((5,)),
            dma((7,)),
            dma((9,)),
        ],
        compiler_params=pltpu.CompilerParams(
            collective_id=0, has_side_effects=True, vmem_limit_bytes=58 * 1024 * 1024
        ),
        cost_estimate=pl.CostEstimate(
            flops=14 * 10**9, bytes_accessed=2 * 10**7, transcendentals=720896
        ),
    )(
        slot_of,
        source_of,
        request,
        enc_gain,
        states,
        queries,
        grad_attn,
        key_weight,
        value_weight,
    )


def body(queries, nb_states, nb_owner, nb_row, enc_gain, key_weight, value_weight, grad_attn):
    groups = lax.axis_size("dp")
    owner_list = nb_owner.reshape(-1)
    row_list = nb_row.reshape(-1)
    asked_count = owner_list.shape[0]
    capacity = 2
    positions = jnp.arange(asked_count, dtype=jnp.int32)
    same_owner = owner_list[:, None] == owner_list[None, :]
    before_me = positions[None, :] < positions[:, None]
    slot_rank = jnp.sum(jnp.where(same_owner & before_me, 1, 0), axis=1).astype(jnp.int32)
    me = lax.axis_index("dp")
    slot_of = lax.rem(owner_list - me - 1 + groups, groups) * capacity + slot_rank
    slot_count = groups * capacity
    slots = jnp.arange(slot_count, dtype=jnp.int32)
    filled = slot_of[:, None] == slots[None, :]
    source_of = asked_count - jnp.sum(
        jnp.where(filled, asked_count - positions[:, None], 0), axis=0
    ).astype(jnp.int32)
    asked_of = owner_list[:, None, None] == jnp.arange(groups, dtype=jnp.int32)[None, :, None]
    rank_is = slot_rank[:, None, None] == jnp.arange(128, dtype=jnp.int32)[None, None, :]
    request = jnp.sum(jnp.where(asked_of & rank_is, row_list[:, None, None], 0), axis=0)
    request = request.astype(jnp.int32).reshape(groups, 1, 128)
    grad_states, attn_out, grad_queries, grad_key_w, grad_value_w = layer(
        slot_of,
        source_of,
        request,
        nb_states,
        queries,
        grad_attn,
        enc_gain,
        key_weight,
        value_weight,
    )
    grad_key_w = grad_key_w.reshape(key_weight.shape)
    grad_value_w = grad_value_w.reshape(value_weight.shape)
    return (attn_out, grad_queries, grad_states, grad_key_w, grad_value_w)


def solution(mesh):
    return jax.shard_map(
        body,
        mesh=mesh,
        in_specs=(
            P("dp", "tensor"),
            P("dp", "tensor", None),
            P("dp", None),
            P("dp", None),
            P(),
            P(None, "tensor"),
            P(None, "tensor"),
            P("dp", "tensor"),
        ),
        out_specs=(
            P("dp", "tensor"),
            P("dp", "tensor"),
            P("dp", "tensor", None),
            P(None, "tensor"),
            P(None, "tensor"),
        ),
        check_vma=False,
    )
```

```python
import jax
import jax.numpy as jnp
from jax import lax
from jax.experimental import pallas as pl
from jax.experimental.pallas import tpu as pltpu
from jax.sharding import PartitionSpec as P

HEAD_DIM = 128
MESH = pl.DeviceIdType.MESH
SCALE = HEAD_DIM ** (-0.5)
RINGS = 4
F32 = jnp.float32
BF16 = jnp.bfloat16

epsilon = 1e-06


def normalize(values):
    widened = values.astype(F32)
    inverse = lax.rsqrt(jnp.mean(widened * widened, axis=-1, keepdims=True) + epsilon)
    return (widened * inverse, inverse)


def dot(a, b, ca, cb):
    return lax.dot_general(a, b, (((ca,), (cb,)), ((), ())), preferred_element_type=F32)


def drain(ref, sem):
    pltpu.make_async_copy(ref, ref, sem).wait()


def send(src, dst, send_sem, recv_sem, device):
    pltpu.make_async_remote_copy(
        src_ref=src,
        dst_ref=dst,
        send_sem=send_sem,
        recv_sem=recv_sem,
        device_id=device,
        device_id_type=MESH,
    ).start()


def layer_kernel(
    spans,
    per,
    places,
    slot_of,
    source_of,
    request,
    gain,
    states_hbm,
    queries_hbm,
    grads_hbm,
    key_w_hbm,
    value_w_hbm,
    grad_states,
    attn_hbm,
    grad_q_hbm,
    grad_key_w_hbm,
    grad_value_w_hbm,
    states,
    queries,
    grads,
    key_w,
    value_w,
    attn_out,
    grad_q,
    grad_key_w,
    grad_value_w,
    asked,
    asked_s,
    stage,
    fetched,
    mine,
    back,
    grad_raw,
    returned,
    slot_rows,
    full,
    enc_t,
    grad_kv,
    term,
    from_core,
    sums,
    near_a,
    near_b,
    far_a,
    far_b,
    w_terms,
    w_big,
    w_mid,
    w_small,
    w_piece,
    w_other,
    w_done,
    w_near,
    w_quarter,
    w_far,
    left_sem,
    right_sem,
    half_sem,
    core_sem,
    swap_sem,
    first_sem,
    second_sem,
    w_sem,
    out_sem,
    swap_out,
    w_out,
    near_sem,
    local_sem,
):
    me_dp = lax.axis_index("dp")
    me_t = lax.axis_index("tensor")
    ring, core = me_t // 2, lax.rem(me_t, 2)
    place, low = me_dp // 2, lax.rem(me_dp, 2)
    r_ring, l_ring, o_ring = (lax.rem(ring + d, RINGS) for d in (1, 3, 2))
    right = {"tensor": r_ring * 2 + core}
    left = {"tensor": l_ring * 2 + core}
    twin = {"tensor": ring * 2 + 1 - core}
    mate = {"dp": place * 2 + 1 - low}
    groups = 2 * places

    y, x = place // 4, lax.rem(place, 4)

    first_at, second_at = (x, y), (y, x)

    def along(axis, d):
        if axis == 0:
            return {"dp": (y * 4 + lax.rem(x + d, 4)) * 2 + low}
        return {"dp": (lax.rem(y + d, 4) * 4 + x) * 2 + low}

    loads = [
        pltpu.make_async_copy(src, dst, local_sem.at[n])
        for n, (src, dst) in enumerate(
            (
                (states_hbm, states),
                (queries_hbm, queries),
                (grads_hbm, grads),
                (key_w_hbm, key_w),
                (value_w_hbm, value_w),
            )
        )
    ]
    stores = [
        pltpu.make_async_copy(src, dst, local_sem.at[5 + n])
        for n, (src, dst) in enumerate(
            (
                (attn_out, attn_hbm),
                (grad_q, grad_q_hbm),
                (grad_key_w, grad_key_w_hbm),
                (grad_value_w, grad_value_w_hbm),
            )
        )
    ]
    for load in loads:
        load.start()

    def ahead(k):
        return {"dp": lax.rem(me_dp + k, groups)}

    def behind(k):
        return {"dp": lax.rem(me_dp + groups - k, groups)}

    barrier = pltpu.get_barrier_semaphore()
    for device in (right, left, twin):
        pl.semaphore_signal(barrier, inc=1, device_id=device, device_id_type=MESH)

    def greet(k, carry):
        pl.semaphore_signal(barrier, inc=1, device_id=ahead(k), device_id_type=MESH)
        return carry

    lax.fori_loop(1, groups, greet, 0)
    pl.semaphore_wait(barrier, 3 + groups - 1)

    def ask(k, carry):
        owner = lax.rem(me_dp + k, groups)
        send(request.at[owner], asked.at[k - 1], near_sem.at[0], near_sem.at[1], ahead(k))
        return carry

    lax.fori_loop(1, groups, ask, 0)
    remote_asked = asked.at[pl.ds(0, groups - 1)]
    asked[groups - 1] = request[me_dp]
    drain(remote_asked, near_sem.at[1])
    to_scalars = pltpu.make_async_copy(asked, asked_s, near_sem.at[2])
    to_scalars.start()
    to_scalars.wait()

    width = states.shape[2]
    others = pl.ds(0, 2 * (groups - 1))
    loads[0].wait()

    def answer(k, carry):
        for r in range(2):
            stage[2 * (k - 1) + r] = states[asked_s[k - 1, 0, r]]
        at = pl.ds(2 * (k - 1), 2)
        send(stage.at[at], fetched.at[at], near_sem.at[3], near_sem.at[4], behind(k))
        return carry

    lax.fori_loop(1, groups, answer, 0)
    for r in range(2):
        fetched[2 * (groups - 1) + r] = states[asked_s[groups - 1, 0, r]]
    for load in loads[1:]:
        load.wait()
    drain(fetched.at[others], near_sem.at[4])

    gain_row = gain[...].reshape(1, width)
    span_len = queries.shape[0] // spans
    local_len = states.shape[1]
    tokens = per * 2 * RINGS * local_len
    cols = queries.shape[1]

    def rows_of(c):
        return pl.ds(c * per, per)

    early = spans // 2 + 1

    def encoder_term(c):
        t_rows = pl.ds(pl.multiple_of(c * tokens, tokens), tokens)
        product = dot(grad_kv[t_rows, :cols], key_w[...], 1, 1)
        product = product + dot(grad_kv[t_rows, cols:], value_w[...], 1, 1)
        at = rows_of(c)
        term[at] = product.astype(BF16).reshape(per, RINGS, 2, local_len, width)
        send(
            term.at[at, :, 1 - core],
            from_core.at[at],
            swap_out.at[0],
            swap_sem.at[c],
            twin,
        )

    def gather_step(i, carry):
        @pl.when(i < spans)
        def _():
            at = rows_of(i)
            for n in range(per):
                mine[i * per + n] = fetched[slot_of[i * per + n]]
            here = full.at[at, ring, core]
            block = mine.at[at]
            send(block, here, out_sem.at[0], left_sem.at[i], right)
            send(block, here, out_sem.at[1], right_sem.at[i], left)
            send(block, here, out_sem.at[2], core_sem.at[i], twin)
            full[at, ring, core] = mine[at]

        j = i - 2

        @pl.when((j >= 0) & (j < spans))
        def _():
            at = rows_of(j)
            from_left = full.at[at, l_ring, core]
            from_right = full.at[at, r_ring, core]
            drain(from_left, left_sem.at[j])
            one = full.at[j * per, l_ring, core]
            send(one, one, out_sem.at[3], half_sem.at[j], right)
            drain(from_right, right_sem.at[j])
            two = full.at[j * per + 1, r_ring, core]
            send(two, two, out_sem.at[4], half_sem.at[j], left)
            send(from_left, from_left, out_sem.at[5], core_sem.at[j], twin)
            send(from_right, from_right, out_sem.at[6], core_sem.at[j], twin)

        k = i - 4

        @pl.when((k >= 0) & (k < spans))
        def _():
            across = full.at[rows_of(k), o_ring, core]
            drain(across, half_sem.at[k])
            send(across, across, out_sem.at[7], core_sem.at[k], twin)

        c = i - 5

        @pl.when(c >= 0)
        def _():
            at = rows_of(c)
            drain(full.at[at, :, 1 - core], core_sem.at[c])
            raw = full[at].reshape(tokens, width)
            unit, _ = normalize(raw)
            encoded = (unit * gain_row).astype(BF16)
            enc_t[:, pl.ds(pl.multiple_of(c * tokens, tokens), tokens)] = encoded.T
            keys = dot(encoded, key_w[...], 1, 0).astype(BF16)
            values = dot(encoded, value_w[...], 1, 0).astype(BF16)
            q_rows = pl.ds(pl.multiple_of(c * span_len, span_len), span_len)
            t_rows = pl.ds(pl.multiple_of(c * tokens, tokens), tokens)
            for h in range(cols // HEAD_DIM):
                lanes = slice(h * HEAD_DIM, (h + 1) * HEAD_DIM)
                q, g = queries[q_rows, lanes], grads[q_rows, lanes]
                kh, vh = keys[:, lanes], values[:, lanes]
                exponent = jnp.exp(dot(q, kh, 1, 1) * SCALE)
                p = exponent / jnp.sum(exponent, axis=-1, keepdims=True)
                w = p.astype(BF16)
                attn_out[q_rows, lanes] = dot(w, vh, 1, 0).astype(BF16)
                gw = dot(g, vh, 1, 1)
                gs = (p * (gw - jnp.sum(p * gw, axis=-1, keepdims=True)) * SCALE).astype(BF16)
                grad_q[q_rows, lanes] = dot(gs, kh, 1, 0).astype(BF16)
                grad_kv[t_rows, lanes] = dot(gs, q, 0, 0).astype(BF16)
                v_lanes = slice(cols + h * HEAD_DIM, cols + (h + 1) * HEAD_DIM)
                grad_kv[t_rows, v_lanes] = dot(w, g, 0, 0).astype(BF16)

        @pl.when((c >= 0) & (c < early))
        def _():
            encoder_term(c)

        return carry

    lax.fori_loop(0, spans + 5, gather_step, 0)
    stores[0].start()
    stores[1].start()

    tile = 256
    tiles = width // tile

    def weight_tile(n):
        part = n // tiles
        r = lax.rem(n, tiles)
        left_side = enc_t[pl.ds(pl.multiple_of(r * tile, tile), tile), :]
        lanes = pl.ds(pl.multiple_of(part * cols, cols), cols)
        row = pl.multiple_of(n * tile, tile)
        w_terms[pl.ds(row, tile), :] = dot(left_side, grad_kv[:, lanes], 1, 0).astype(BF16)

    quarter = width // 4
    piece = quarter // 4

    def quarter_rows(part, a):
        return pl.ds(pl.multiple_of(part * width + a * quarter, quarter), quarter)

    def reduce_step(i, carry):
        @pl.when((i >= early) & (i < spans))
        def _():
            encoder_term(i)

        j = i - 1

        @pl.when((j >= 0) & (j < spans))
        def _():
            at = rows_of(j)
            drain(from_core.at[at], swap_sem.at[j])
            total = term[at, :, core].astype(F32) + from_core[at].astype(F32)
            sums[at] = total.astype(BF16)
            send(sums.at[j * per, o_ring], near_a.at[j], swap_out.at[1], first_sem.at[0, j], right)
            send(
                sums.at[j * per + 1, o_ring], near_b.at[j], swap_out.at[2], first_sem.at[1, j], left
            )

        k = i - 3

        @pl.when((k >= 0) & (k < spans))
        def _():
            at = rows_of(k)
            drain(near_a.at[k], first_sem.at[0, k])
            total = sums[k * per, r_ring].astype(F32) + near_a[k].astype(F32)
            sums[k * per, r_ring] = total.astype(BF16)
            send(sums.at[at, r_ring], far_a.at[at], swap_out.at[3], second_sem.at[0, k], right)
            drain(near_b.at[k], first_sem.at[1, k])
            total = sums[k * per + 1, l_ring].astype(F32) + near_b[k].astype(F32)
            sums[k * per + 1, l_ring] = total.astype(BF16)
            send(sums.at[at, l_ring], far_b.at[at], swap_out.at[4], second_sem.at[1, k], left)

        @pl.when((i == 2) | (i == 3))
        def _():
            def tile_step(n, carry):
                weight_tile(tiles * (i - 2) + n)
                return carry

            lax.fori_loop(0, tiles, tile_step, 0)

        @pl.when(i == 3)
        def _():
            for d in (1, 2, 3):
                for part in range(2):
                    send(
                        w_terms.at[quarter_rows(part, lax.rem(first_at[part] + d, 4))],
                        w_big.at[part, d - 1],
                        w_out.at[0],
                        w_sem.at[0],
                        along(part, d),
                    )

        @pl.when(i == 7)
        def _():
            drain(w_big, w_sem.at[0])
            for part in range(2):
                total = w_terms[quarter_rows(part, first_at[part]), :].astype(F32)
                for d in range(3):
                    total = total + w_big[part, d].astype(F32)
                w_mid[part] = total.astype(BF16).reshape(4, piece, cols)
                for d in (1, 2, 3):
                    send(
                        w_mid.at[part, lax.rem(second_at[part] + d, 4)],
                        w_small.at[part, d - 1],
                        w_out.at[1],
                        w_sem.at[1],
                        along(1 - part, d),
                    )

        @pl.when(i == 8)
        def _():
            drain(w_small, w_sem.at[1])
            for part in range(2):
                total = w_mid[part, second_at[part]].astype(F32)
                for d in range(3):
                    total = total + w_small[part, d].astype(F32)
                w_piece[part] = total.astype(BF16)
            send(w_piece, w_other, w_out.at[2], w_sem.at[2], mate)

        @pl.when(i == 9)
        def _():
            drain(w_other, w_sem.at[2])
            for part in range(2):
                total = w_piece[part].astype(F32) + w_other[part].astype(F32)
                w_done[part] = total.astype(BF16)
                w_quarter[part, second_at[part]] = total.astype(BF16)
                for d in (1, 2, 3):
                    send(
                        w_done.at[part],
                        w_near.at[part, d - 1],
                        w_out.at[3],
                        w_sem.at[3],
                        along(1 - part, d),
                    )

        @pl.when(i == 10)
        def _():
            drain(w_near, w_sem.at[3])
            for part in range(2):
                for d in (1, 2, 3):
                    w_quarter[part, lax.rem(second_at[part] + 4 - d, 4)] = w_near[part, d - 1]
                for d in (1, 2, 3):
                    send(
                        w_quarter.at[part],
                        w_far.at[part, d - 1],
                        w_out.at[4],
                        w_sem.at[4],
                        along(part, d),
                    )

        c = i - 5

        @pl.when(c >= 0)
        def _():
            at = rows_of(c)
            drain(far_a.at[at], second_sem.at[0, c])
            drain(far_b.at[at], second_sem.at[1, c])
            own = sums[at, ring].astype(F32) + far_a[at].astype(F32) + far_b[at].astype(F32)
            own = own.reshape(per * local_len, width)
            unit, inverse = normalize(mine[at].reshape(per * local_len, width))
            scaled = own * gain_row
            raw = inverse * (scaled - unit * jnp.mean(scaled * unit, axis=-1, keepdims=True))
            grad_raw[at] = raw.astype(BF16).reshape(per, local_len, width)

        return carry

    lax.fori_loop(0, spans + 5, reduce_step, 0)

    asked_count = spans * per
    grad_raw[asked_count] = jnp.zeros((local_len, width), BF16)

    def give_back(k, carry):
        for r in range(2):
            back[2 * (k - 1) + r] = grad_raw[source_of[2 * (k - 1) + r]]
        at = pl.ds(2 * (k - 1), 2)
        send(back.at[at], returned.at[at], near_sem.at[5], near_sem.at[6], ahead(k))
        return carry

    lax.fori_loop(1, groups, give_back, 0)
    for r in range(2):
        returned[2 * (groups - 1) + r] = grad_raw[source_of[2 * (groups - 1) + r]]

    def name_rows(k, carry):
        for r in range(2):
            rows = pl.ds(pl.multiple_of((2 * k + r) * local_len, local_len), local_len)
            slot_rows[rows, :] = jnp.full((local_len, 256), asked_s[k, 0, r], jnp.int32)
        return carry

    lax.fori_loop(0, groups, name_rows, 0)

    drain(w_far, w_sem.at[4])
    for part, out in enumerate((grad_key_w, grad_value_w)):
        out[first_at[part]] = w_quarter[part].reshape(quarter, cols).astype(F32)
        for d in (1, 2, 3):
            value = w_far[part, d - 1].reshape(quarter, cols).astype(F32)
            out[lax.rem(first_at[part] + 4 - d, 4)] = value
        stores[2 + part].start()

    slot_tokens = 2 * groups * local_len
    owned = states.shape[0] * local_len
    shape = (slot_tokens, owned)
    to_row = lax.broadcasted_iota(jnp.int32, shape, 1)
    token = lax.broadcasted_iota(jnp.int32, shape, 0)
    wanted = slot_rows[...] * local_len + lax.rem(token, local_len)
    chosen = jnp.where(wanted == to_row, 1.0, 0.0).astype(BF16)
    drain(returned.at[others], near_sem.at[6])
    total = dot(chosen, returned[...].reshape(slot_tokens, width), 0, 0)
    grad_states[...] = total.astype(BF16).reshape(states.shape)

    drain(remote_asked, near_sem.at[0])
    drain(stage.at[others], near_sem.at[3])
    drain(back.at[others], near_sem.at[5])
    few = mine.at[pl.ds(0, spans)]
    for n in (0, 1, 2, 5, 6, 7):
        drain(mine, out_sem.at[n])
    drain(few, out_sem.at[3])
    drain(few, out_sem.at[4])
    drain(from_core, swap_out.at[0])
    drain(near_a, swap_out.at[1])
    drain(near_b, swap_out.at[2])
    drain(far_a, swap_out.at[3])
    drain(far_b, swap_out.at[4])
    for n, ref in enumerate((w_big, w_small, w_other, w_near, w_far)):
        drain(ref, w_out.at[n])
    for store in stores:
        store.wait()


def layer(
    slot_of, source_of, request, states, queries, grad_attn, enc_gain, key_weight, value_weight
):
    groups = request.shape[0]
    owned, local_len, width = states.shape
    asked = slot_of.shape[0]
    per = 2
    spans = asked // per
    rows, cols = queries.shape
    places = groups // 2
    tokens = asked * local_len * RINGS * 2
    quarter, piece = width // 4, width // 16

    def kernel(*refs):
        layer_kernel(spans, per, places, *refs)

    vmem = pl.BlockSpec(memory_space=pltpu.VMEM)
    smem = pl.BlockSpec(memory_space=pltpu.SMEM)
    anywhere = pl.BlockSpec(memory_space=pl.ANY)
    dma = pltpu.SemaphoreType.DMA
    return pl.pallas_call(
        kernel,
        out_shape=(
            jax.ShapeDtypeStruct((owned, local_len, width), BF16),
            jax.ShapeDtypeStruct((rows, cols), BF16),
            jax.ShapeDtypeStruct((rows, cols), BF16),
            jax.ShapeDtypeStruct((4, quarter, cols), F32),
            jax.ShapeDtypeStruct((4, quarter, cols), F32),
        ),
        in_specs=[smem] * 2 + [vmem] * 2 + [anywhere] * 5,
        out_specs=(vmem,) + (anywhere,) * 4,
        scratch_shapes=[
            pltpu.VMEM((owned, local_len, width), BF16),
            pltpu.VMEM((rows, cols), BF16),
            pltpu.VMEM((rows, cols), BF16),
            pltpu.VMEM((width, cols), BF16),
            pltpu.VMEM((width, cols), BF16),
            pltpu.VMEM((rows, cols), BF16),
            pltpu.VMEM((rows, cols), BF16),
            pltpu.VMEM((4, quarter, cols), F32),
            pltpu.VMEM((4, quarter, cols), F32),
            pltpu.VMEM((groups, 1, 128), jnp.int32),
            pltpu.SMEM((groups, 1, 128), jnp.int32),
            pltpu.VMEM((2 * groups, local_len, width), BF16),
            pltpu.VMEM((2 * groups, local_len, width), BF16),
            pltpu.VMEM((asked, local_len, width), BF16),
            pltpu.VMEM((2 * groups, local_len, width), BF16),
            pltpu.VMEM((asked + 1, local_len, width), BF16),
            pltpu.VMEM((2 * groups, local_len, width), BF16),
            pltpu.VMEM((2 * groups * local_len, owned * local_len), jnp.int32),
            pltpu.VMEM((asked, RINGS, 2, local_len, width), BF16),
            pltpu.VMEM((width, tokens), BF16),
            pltpu.VMEM((tokens, 2 * cols), BF16),
            pltpu.VMEM((asked, RINGS, 2, local_len, width), BF16),
            pltpu.VMEM((asked, RINGS, local_len, width), BF16),
            pltpu.VMEM((asked, RINGS, local_len, width), BF16),
            pltpu.VMEM((spans, local_len, width), BF16),
            pltpu.VMEM((spans, local_len, width), BF16),
            pltpu.VMEM((asked, local_len, width), BF16),
            pltpu.VMEM((asked, local_len, width), BF16),
            pltpu.VMEM((2 * width, cols), BF16),
            pltpu.VMEM((2, 3, quarter, cols), BF16),
            pltpu.VMEM((2, 4, piece, cols), BF16),
            pltpu.VMEM((2, 3, piece, cols), BF16),
            pltpu.VMEM((2, piece, cols), BF16),
            pltpu.VMEM((2, piece, cols), BF16),
            pltpu.VMEM((2, piece, cols), BF16),
            pltpu.VMEM((2, 3, piece, cols), BF16),
            pltpu.VMEM((2, 4, piece, cols), BF16),
            pltpu.VMEM((2, 3, 4, piece, cols), BF16),
            dma((spans,)),
            dma((spans,)),
            dma((spans,)),
            dma((spans,)),
            dma((spans,)),
            dma((2, spans)),
            dma((2, spans)),
            dma((5,)),
            dma((8,)),
            dma((5,)),
            dma((5,)),
            dma((7,)),
            dma((9,)),
        ],
        compiler_params=pltpu.CompilerParams(
            collective_id=0, has_side_effects=True, vmem_limit_bytes=58 * 1024 * 1024
        ),
        cost_estimate=pl.CostEstimate(
            flops=14 * 10**9, bytes_accessed=2 * 10**7, transcendentals=720896
        ),
    )(
        slot_of,
        source_of,
        request,
        enc_gain,
        states,
        queries,
        grad_attn,
        key_weight,
        value_weight,
    )


def body(queries, nb_states, nb_owner, nb_row, enc_gain, key_weight, value_weight, grad_attn):
    groups = lax.axis_size("dp")
    owner_list = nb_owner.reshape(-1)
    row_list = nb_row.reshape(-1)
    asked_count = owner_list.shape[0]
    capacity = 2
    positions = jnp.arange(asked_count, dtype=jnp.int32)
    same_owner = owner_list[:, None] == owner_list[None, :]
    before_me = positions[None, :] < positions[:, None]
    slot_rank = jnp.sum(jnp.where(same_owner & before_me, 1, 0), axis=1).astype(jnp.int32)
    me = lax.axis_index("dp")
    slot_of = lax.rem(owner_list - me - 1 + groups, groups) * capacity + slot_rank
    slot_count = groups * capacity
    slots = jnp.arange(slot_count, dtype=jnp.int32)
    filled = slot_of[:, None] == slots[None, :]
    source_of = asked_count - jnp.sum(
        jnp.where(filled, asked_count - positions[:, None], 0), axis=0
    ).astype(jnp.int32)
    asked_of = owner_list[:, None, None] == jnp.arange(groups, dtype=jnp.int32)[None, :, None]
    rank_is = slot_rank[:, None, None] == jnp.arange(128, dtype=jnp.int32)[None, None, :]
    request = jnp.sum(jnp.where(asked_of & rank_is, row_list[:, None, None], 0), axis=0)
    request = request.astype(jnp.int32).reshape(groups, 1, 128)
    grad_states, attn_out, grad_queries, grad_key_w, grad_value_w = layer(
        slot_of,
        source_of,
        request,
        nb_states,
        queries,
        grad_attn,
        enc_gain,
        key_weight,
        value_weight,
    )
    grad_key_w = grad_key_w.reshape(key_weight.shape)
    grad_value_w = grad_value_w.reshape(value_weight.shape)
    return (attn_out, grad_queries, grad_states, grad_key_w, grad_value_w)


def solution(mesh):
    return jax.shard_map(
        body,
        mesh=mesh,
        in_specs=(
            P("dp", "tensor"),
            P("dp", "tensor", None),
            P("dp", None),
            P("dp", None),
            P(),
            P(None, "tensor"),
            P(None, "tensor"),
            P("dp", "tensor"),
        ),
        out_specs=(
            P("dp", "tensor"),
            P("dp", "tensor"),
            P("dp", "tensor", None),
            P(None, "tensor"),
            P(None, "tensor"),
        ),
        check_vma=False,
    )
```
